32 devices in a mesh: dp: 4 (over x, core), group: 8 (over z, y).
Axes of the slice: x: 2, y: 2, z: 4, core: 2. Of those that a mesh axis runs over, the one named last changes fastest.
Arguments:
- embeds: bfloat16 [8192, 1024], P(('dp', 'group')), may hold values from -6 to 6
- row_ids: int32 [8192], P(('dp', 'group')), may hold values from 0 to 63
- neighbors: int32 [32, 3], P('dp'), may hold values from 0 to 7, as said below
- w_first: bfloat16 [1024, 4096], P(None, 'dp'), may hold values from -0.1875 to 0.1875
- w_second: bfloat16 [4096, 1024], P('dp'), may hold values from -0.09375 to 0.09375
Outputs:
- grad_first: float32 [1024, 4096], P('group', 'dp')
- grad_second: float32 [4096, 1024], P('dp', 'group')
- grad_unit: float32 [8192, 1024], P(('dp', 'group'))
The draws below stay inside these ranges and needn't reach their ends.
Inputs may be any that keep to these rules, and one draw needn't show every extreme that they name: `neighbors`: within a row the 3 entries differ from one another and from the row's own index b % 8.
All inputs are finite; a program needn't handle non-finite values.
Results may differ from the reference program's by a relative error of at most 0.013.
Values may be sent and summed in bfloat16 or wider, within the bound.
A program may use at most 64 MiB of HBM per device.

```python
import jax
import jax.numpy as jnp
from jax import lax

E = 1024
H = 4096
P_SIZE = 1024
BLOCK = 256
K = 3
CLASSES = 64
OWNERS = 8
N_BLOCKS = 32
ROWS = 8192
N_DP = 4


CLASS_SHARE = 0.6


LATENT_SHARE = 0.8


def shared_trace_ids(key):
    return jax.random.randint(jax.random.fold_in(key, 11), (ROWS,), 0, CLASSES).astype(jnp.int32)


def draw_row_ids(key, part):
    return shared_trace_ids(key)


def draw_embeds(key, part):
    trace_ids = shared_trace_ids(key)
    streams = jax.random.split(jax.random.fold_in(key, 23), 4)
    latent = jax.random.normal(streams[0], (CLASSES, 4), jnp.float32)
    squares = latent * latent
    length = squares[:, 0] + squares[:, 1] + squares[:, 2] + squares[:, 3]
    latent = latent * lax.rsqrt(jnp.maximum(length, 0.0001))[:, None]
    basis = jax.random.normal(streams[1], (4, E), jnp.float32)
    mixed = latent[:, 0:1] * basis[0][None, :] + latent[:, 1:2] * basis[1][None, :] + latent[:, 2:3] * basis[2][None, :] + latent[:, 3:4] * basis[3][None, :]
    apart = jax.random.normal(streams[2], (CLASSES, E), jnp.float32)
    classes = jnp.sqrt(LATENT_SHARE) * mixed + jnp.sqrt(1.0 - LATENT_SHARE) * apart
    noise = jax.random.normal(streams[3], (ROWS, E), jnp.float32)
    class_rows = jnp.take(classes, trace_ids, axis=0)
    values = jnp.sqrt(1.0 - CLASS_SHARE) * noise + jnp.sqrt(CLASS_SHARE) * class_rows
    return jnp.clip(values, -6.0, 6.0).astype(jnp.bfloat16)


def draw_neighbors(key, part):
    key_pop, key_noise = jax.random.split(jax.random.fold_in(key, 17))
    slices = N_BLOCKS // OWNERS
    popular = jax.random.randint(key_pop, (slices, 1, OWNERS), 0, 4)
    noise = jax.random.randint(key_noise, (slices, OWNERS, OWNERS), 0, 65536)
    target = jnp.arange(OWNERS, dtype=jnp.int32)
    priority = (popular * 65536 + noise) * OWNERS + target[None, None, :]
    own = target[:, None] == target[None, :]
    priority = jnp.where(own[None], -1, priority)
    _, chosen = lax.top_k(priority, K)
    return chosen.reshape(N_BLOCKS, K).astype(jnp.int32)


def shard_levels(stream_key, extent, cuts, least, top_value):
    gain, own = 1.0, jax.random.fold_in(stream_key, 6)
    for dim, shards_of in cuts:
        steps = jnp.exp(jax.random.uniform(jax.random.fold_in(own, dim), (shards_of,), jnp.float32, least / len(cuts), top_value / len(cuts)))
        gain = gain * jnp.repeat(steps, extent[dim] // shards_of).reshape([-1 if axis == dim else 1 for axis in range(len(extent))])
    return gain


def bell_draw(key, extent, width, bound, cuts=(), kind=jnp.bfloat16):
    array = jax.random.normal(key, extent, jnp.float32) * width
    if len(cuts) > 0:
        array = shard_levels(key, extent, cuts, -0.22, 0.18) * array
    return jnp.clip(array, min=-bound, max=bound).astype(kind)


def setup_inputs(seed: int = 0) -> dict:
    seeds = jax.random.split(jax.random.key(seed), 6)
    return {
        "embeds": draw_embeds(jax.random.fold_in(seeds[5], 71), 0),
        "row_ids": draw_row_ids(jax.random.fold_in(seeds[5], 71), 0),
        "neighbors": draw_neighbors(jax.random.fold_in(seeds[5], 71), 0),
        "w_first": bell_draw(seeds[3], (E, H), E ** -0.5, 0.1875, ((1, 4),)),
        "w_second": bell_draw(seeds[4], (H, P_SIZE), H ** -0.5, 0.09375, ((0, 4),)),
    }


EPS = 1e-06
TEMP = 10.0
SHIFT = -5.0

def gelu_fwd(value):
    return jax.nn.gelu(value, approximate=True)

def gelu_back(pre, grad):
    _, back = jax.vjp(gelu_fwd, pre)
    return back(grad)[0]

def block_terms(own, own_ids, cand, cand_ids):
    logits = TEMP / P_SIZE * jnp.einsum('rp,kcp->krc', own, cand) + SHIFT
    sign = jnp.where(own_ids[None, :, None] == cand_ids[:, None, :], 1.0, -1.0).astype(jnp.float32)
    weight = (-sign * jax.nn.sigmoid(-sign * logits) * (TEMP / P_SIZE)).astype(jnp.bfloat16)
    weight = lax.optimization_barrier(weight).astype(jnp.float32)
    grad_own = jnp.einsum('krc,kcp->rp', weight, cand)
    grad_cand = jnp.einsum('krc,rp->kcp', weight, own)
    return (grad_own, grad_cand)

def slice_terms(inputs):
    units, ids, lists = inputs

    def one_block(inner):
        own, own_ids, listed = inner
        cand = jnp.concatenate([own[None], jnp.take(units, listed, axis=0)], 0).astype(jnp.float32)
        cand_ids = jnp.concatenate([own_ids[None], jnp.take(ids, listed, axis=0)], 0)
        return block_terms(own.astype(jnp.float32), own_ids, cand, cand_ids)
    grad_own, grad_cand = lax.map(one_block, (units, ids, lists))
    returned = jnp.zeros((OWNERS, BLOCK, P_SIZE), jnp.float32).at[lists.reshape(-1)].add(grad_cand[:, 1:].reshape(-1, BLOCK, P_SIZE))
    return grad_own + grad_cand[:, 0] + returned

def reference(embeds, row_ids, neighbors, w_first, w_second):
    share = H // N_DP
    proj = jnp.zeros((ROWS, P_SIZE), jnp.float32)
    for index in range(N_DP):
        pre = jnp.dot(embeds, w_first[:, index * share:(index + 1) * share], preferred_element_type=jnp.float32)
        hidden = gelu_fwd(pre).astype(jnp.bfloat16)
        part = jnp.dot(hidden, w_second[index * share:(index + 1) * share], preferred_element_type=jnp.float32)
        part = lax.optimization_barrier(part.astype(jnp.bfloat16)).astype(jnp.float32)
        proj = proj + part
    inv = lax.rsqrt(lax.optimization_barrier(jnp.mean(proj * proj, axis=-1, keepdims=True)) + EPS)
    unit = proj * inv
    unit_b = unit.astype(jnp.bfloat16)
    grad_unit = lax.map(slice_terms, (unit_b.reshape(N_DP, OWNERS, BLOCK, P_SIZE), row_ids.reshape(N_DP, OWNERS, BLOCK), neighbors.reshape(N_DP, OWNERS, K)))
    grad_unit = grad_unit.reshape(ROWS, P_SIZE)
    grad_proj = (inv * (grad_unit - unit * lax.optimization_barrier(jnp.mean(unit * grad_unit, axis=-1, keepdims=True)))).astype(jnp.bfloat16)
    firsts = []
    seconds = []
    for index in range(N_DP):
        w_part = w_second[index * share:(index + 1) * share]
        pre = jnp.dot(embeds, w_first[:, index * share:(index + 1) * share], preferred_element_type=jnp.float32)
        hidden = gelu_fwd(pre).astype(jnp.bfloat16)
        seconds.append(jnp.dot(hidden.T, grad_proj, preferred_element_type=jnp.float32))
        grad_hidden = jnp.dot(grad_proj, w_part.T, preferred_element_type=jnp.float32)
        grad_pre = gelu_back(pre, grad_hidden).astype(jnp.bfloat16)
        firsts.append(jnp.dot(embeds.T, grad_pre, preferred_element_type=jnp.float32))
    return (jnp.concatenate(firsts, 1), jnp.concatenate(seconds, 0), grad_unit)
```

```python
import jax
import jax.numpy as jnp
from jax import lax
from jax.sharding import PartitionSpec as P

EPS = 1e-06
TEMP = 10.0
SHIFT = -5.0


def gelu_fwd(value):
    return jax.nn.gelu(value, approximate=True)


def gelu_back(pre, grad):
    _, back = jax.vjp(gelu_fwd, pre)
    return back(grad)[0]


def per_device(embeds, row_ids, neighbors, w_first, w_second):
    owners = lax.axis_size("group")
    block = embeds.shape[0]
    width = w_second.shape[1]
    gathered = lax.all_gather(embeds, "dp", axis=0, tiled=True)
    pre = jnp.dot(gathered, w_first, preferred_element_type=jnp.float32)
    hidden = gelu_fwd(pre).astype(jnp.bfloat16)
    proj = lax.psum_scatter(
        jnp.dot(hidden, w_second, preferred_element_type=jnp.float32).astype(jnp.bfloat16),
        "dp",
        scatter_dimension=0,
        tiled=True,
    ).astype(jnp.float32)
    inv = lax.rsqrt(jnp.mean(proj * proj, axis=-1, keepdims=True) + EPS)
    unit = proj * inv
    unit_b = unit.astype(jnp.bfloat16)
    units = lax.all_gather(unit_b, "group", axis=0, tiled=True)
    ids = lax.all_gather(row_ids, "group", axis=0, tiled=True)
    me = lax.axis_index("group")
    others = jnp.arange(owners, dtype=jnp.int32)
    mine = lax.dynamic_index_in_dim(neighbors, me, 0, keepdims=False)
    lists = jnp.sum((mine[None, :] == others[:, None]).astype(jnp.float32), axis=1)
    listed_by = jnp.sum((neighbors == me).astype(jnp.float32), axis=1)
    times = jnp.where(others == me, 2.0, lists + listed_by)
    times = jnp.repeat(times, block)[None, :]
    logits = (
        TEMP
        / width
        * lax.dot_general(
            unit_b, units, (((1,), (1,)), ((), ())), preferred_element_type=jnp.float32
        )
        + SHIFT
    )
    sign = jnp.where(row_ids[:, None] == ids[None, :], 1.0, -1.0).astype(jnp.float32)
    weight = (-sign * jax.nn.sigmoid(-sign * logits) * (TEMP / width)).astype(jnp.bfloat16)
    weight = weight * times.astype(jnp.bfloat16)
    grad_unit = jnp.dot(weight, units, preferred_element_type=jnp.float32)
    grad_proj = inv * (grad_unit - unit * jnp.mean(unit * grad_unit, axis=-1, keepdims=True))
    grad_all = lax.all_gather(grad_proj.astype(jnp.bfloat16), "dp", axis=0, tiled=True)
    second_local = lax.dot_general(
        hidden, grad_all, (((0,), (0,)), ((), ())), preferred_element_type=jnp.float32
    )
    grad_hidden = lax.dot_general(
        grad_all, w_second, (((1,), (1,)), ((), ())), preferred_element_type=jnp.float32
    )
    grad_pre = gelu_back(pre, grad_hidden).astype(jnp.bfloat16)
    first_local = lax.dot_general(
        gathered, grad_pre, (((0,), (0,)), ((), ())), preferred_element_type=jnp.float32
    )
    first_out, second_out = (
        lax.psum_scatter(first_local, "group", scatter_dimension=0, tiled=True),
        lax.psum_scatter(second_local, "group", scatter_dimension=1, tiled=True),
    )
    return (first_out, second_out, grad_unit)


def solution(mesh):
    in_specs = (
        P(("dp", "group"), None),
        P(("dp", "group")),
        P("dp", None),
        P(None, "dp"),
        P("dp", None),
    )
    out_specs = (P("group", "dp"), P("dp", "group"), P(("dp", "group"), None))
    return jax.shard_map(
        per_device, mesh=mesh, in_specs=in_specs, out_specs=out_specs, check_vma=False
    )
```

```python
import functools

import jax
import jax.numpy as jnp
from jax import lax
from jax.experimental import pallas as pl
from jax.experimental.pallas import tpu as pltpu
from jax.sharding import PartitionSpec as P

EPS = 1e-06
TEMP = 10.0
SHIFT = -5.0
LEVELS = 32000.0
LANES = 128
CHUNK = 256
VMEM_BYTES = 60 * 1024 * 1024
MESH = pl.DeviceIdType.MESH


def gelu_fwd(value):
    return jax.nn.gelu(value, approximate=True)


def gelu_back(pre, grad):
    _, back = jax.vjp(gelu_fwd, pre)
    return back(grad)[0]


def encode(value):
    flat = value.reshape(-1, value.shape[-1])
    top = jnp.max(jnp.abs(flat), axis=0, keepdims=True)
    joint = top[:, :LANES]
    for at in range(LANES, top.shape[1], LANES):
        joint = jnp.maximum(joint, top[:, at : at + LANES])
    joint = jnp.maximum(joint, 1e-30)
    inverse = jnp.tile(LEVELS / joint, (1, top.shape[1] // LANES))
    code = jnp.round(flat * inverse).astype(jnp.int32).astype(jnp.int16)
    return code.reshape(value.shape), jnp.broadcast_to(joint * (1.0 / LEVELS), (8, LANES))


def decode(code, scale):
    wide = jnp.tile(scale[0:1], (1, code.shape[-1] // LANES))
    return code.astype(jnp.int32).astype(jnp.float32) * wide


def weight_kernel(
    n_y,
    n_z,
    left0,
    left1,
    right0,
    right1,
    out,
    own,
    mine,
    y_out,
    y_in,
    y_scale_out,
    y_scale_in,
    z_out,
    z_in,
    z_scale_out,
    z_scale_in,
    y_sems,
    z_sems,
):
    me = lax.axis_index("group")
    z, y = me // n_y, me % n_y
    tall = out.shape[1]
    chunks = out.shape[2] // CHUNK

    def y_peer(d):
        return z * n_y + lax.rem(y + d, n_y)

    def z_peer(d):
        return lax.rem(z + d, n_z) * n_y + y

    def y_copies(i, d):
        return [
            pltpu.make_async_remote_copy(
                src_ref=a.at[i, d - 1],
                dst_ref=b.at[i, d - 1],
                send_sem=y_sems.at[which, 0, i, d - 1],
                recv_sem=y_sems.at[which, 1, i, d - 1],
                device_id={"group": y_peer(d)},
                device_id_type=MESH,
            )
            for which, (a, b) in enumerate(((y_out, y_in), (y_scale_out, y_scale_in)))
        ]

    def z_copies(i, d):
        return [
            pltpu.make_async_remote_copy(
                src_ref=a.at[i, d - 1],
                dst_ref=b.at[i, d - 1],
                send_sem=z_sems.at[which, 0, i, d - 1],
                recv_sem=z_sems.at[which, 1, i, d - 1],
                device_id={"group": z_peer(d)},
                device_id_type=MESH,
            )
            for which, (a, b) in enumerate(((z_out, z_in), (z_scale_out, z_scale_in)))
        ]

    barrier = pltpu.get_barrier_semaphore()
    for d in range(1, n_y):
        pl.semaphore_signal(barrier, inc=1, device_id={"group": y_peer(d)}, device_id_type=MESH)
    for d in range(1, n_z):
        pl.semaphore_signal(barrier, inc=1, device_id={"group": z_peer(d)}, device_id_type=MESH)
    pl.semaphore_wait(barrier, n_y + n_z - 2)

    for m, (left, right) in enumerate(((left0, right0), (left1, right1))):

        @pl.loop(0, chunks)
        def _(k, m=m, left=left, right=right):
            i = m * chunks + k
            columns = pl.ds(pl.multiple_of(k * CHUNK, CHUNK), CHUNK)
            rhs = right[:, columns]

            def partial(owner_y, row):
                at = pl.multiple_of((row * n_y + owner_y) * tall, tall)
                return jnp.dot(
                    left[pl.ds(at, tall), :], rhs, preferred_element_type=jnp.float32
                )

            for d in range(1, n_y):
                blocks = jnp.stack([partial(lax.rem(y + d, n_y), row) for row in range(n_z)])
                code, scale = encode(blocks)
                y_out[i, d - 1] = code
                y_scale_out[i, d - 1] = scale
                for copy in y_copies(i, d):
                    copy.start()
            for row in range(n_z):
                own[i, row] = partial(y, row)

    @pl.loop(0, 2 * chunks)
    def _(i):
        for d in range(1, n_y):
            for copy in y_copies(i, d):
                copy.wait_recv()
        for d in range(1, n_z):
            row = lax.rem(z + d, n_z)
            block = own[i, row]
            for e in range(1, n_y):
                block = block + decode(y_in[i, e - 1, row], y_scale_in[i, e - 1])
            code, scale = encode(block)
            z_out[i, d - 1] = code
            z_scale_out[i, d - 1] = scale
            for copy in z_copies(i, d):
                copy.start()
        block = own[i, z]
        for e in range(1, n_y):
            block = block + decode(y_in[i, e - 1, z], y_scale_in[i, e - 1])
        mine[i] = block

    for m in range(2):

        @pl.loop(0, chunks)
        def _(k, m=m):
            i = m * chunks + k
            block = mine[i]
            for d in range(1, n_z):
                for copy in z_copies(i, d):
                    copy.wait_recv()
            for d in range(1, n_z):
                block = block + decode(z_in[i, d - 1], z_scale_in[i, d - 1])
            out[m, :, pl.ds(pl.multiple_of(k * CHUNK, CHUNK), CHUNK)] = block

    @pl.loop(0, 2 * chunks)
    def _(i):
        for d in range(1, n_y):
            for copy in y_copies(i, d):
                copy.wait_send()
        for d in range(1, n_z):
            for copy in z_copies(i, d):
                copy.wait_send()


def weight_sums(left0, left1, right0, right1):
    owners, shares = lax.axis_size("group"), lax.axis_size("dp")
    n_y = shares // 2 if owners % (shares // 2) == 0 else 1
    n_z = owners // n_y
    tall = left0.shape[0] // owners
    wide = right0.shape[1]
    items = 2 * (wide // CHUNK)
    vmem = pl.BlockSpec(memory_space=pltpu.VMEM)
    return pl.pallas_call(
        functools.partial(weight_kernel, n_y, n_z),
        out_shape=jax.ShapeDtypeStruct((2, tall, wide), jnp.float32),
        in_specs=[vmem] * 4,
        out_specs=vmem,
        scratch_shapes=[
            pltpu.VMEM((items, n_z, tall, CHUNK), jnp.float32),
            pltpu.VMEM((items, tall, CHUNK), jnp.float32),
            pltpu.VMEM((items, n_y - 1, n_z, tall, CHUNK), jnp.int16),
            pltpu.VMEM((items, n_y - 1, n_z, tall, CHUNK), jnp.int16),
            pltpu.VMEM((items, n_y - 1, 8, LANES), jnp.float32),
            pltpu.VMEM((items, n_y - 1, 8, LANES), jnp.float32),
            pltpu.VMEM((items, n_z - 1, tall, CHUNK), jnp.int16),
            pltpu.VMEM((items, n_z - 1, tall, CHUNK), jnp.int16),
            pltpu.VMEM((items, n_z - 1, 8, LANES), jnp.float32),
            pltpu.VMEM((items, n_z - 1, 8, LANES), jnp.float32),
            pltpu.SemaphoreType.DMA((2, 2, items, n_y - 1)),
            pltpu.SemaphoreType.DMA((2, 2, items, n_z - 1)),
        ],
        compiler_params=pltpu.CompilerParams(
            collective_id=0, has_side_effects=True, vmem_limit_bytes=VMEM_BYTES
        ),
    )(left0, left1, right0, right1)


def per_device(embeds, row_ids, neighbors, w_first, w_second):
    owners = lax.axis_size("group")
    block = embeds.shape[0]
    width = w_second.shape[1]
    gathered = lax.all_gather(embeds, "dp", axis=0, tiled=True)
    pre = jnp.dot(gathered, w_first, preferred_element_type=jnp.float32)
    hidden = gelu_fwd(pre).astype(jnp.bfloat16)
    proj = lax.psum_scatter(
        jnp.dot(hidden, w_second, preferred_element_type=jnp.float32).astype(jnp.bfloat16),
        "dp",
        scatter_dimension=0,
        tiled=True,
    ).astype(jnp.float32)
    inv = lax.rsqrt(jnp.mean(proj * proj, axis=-1, keepdims=True) + EPS)
    unit = proj * inv
    unit_b = unit.astype(jnp.bfloat16)
    units = lax.all_gather(unit_b, "group", axis=0, tiled=True)
    ids = lax.all_gather(row_ids, "group", axis=0, tiled=True)
    me = lax.axis_index("group")
    others = jnp.arange(owners, dtype=jnp.int32)
    mine = lax.dynamic_index_in_dim(neighbors, me, 0, keepdims=False)
    lists = jnp.sum((mine[None, :] == others[:, None]).astype(jnp.float32), axis=1)
    listed_by = jnp.sum((neighbors == me).astype(jnp.float32), axis=1)
    times = jnp.where(others == me, 2.0, lists + listed_by)
    times = jnp.repeat(times, block)[None, :]
    logits = (
        TEMP
        / width
        * lax.dot_general(
            unit_b, units, (((1,), (1,)), ((), ())), preferred_element_type=jnp.float32
        )
        + SHIFT
    )
    sign = jnp.where(row_ids[:, None] == ids[None, :], 1.0, -1.0).astype(jnp.float32)
    weight = (-sign * jax.nn.sigmoid(-sign * logits) * (TEMP / width)).astype(jnp.bfloat16)
    weight = weight * times.astype(jnp.bfloat16)
    grad_unit = jnp.dot(weight, units, preferred_element_type=jnp.float32)
    grad_proj = inv * (grad_unit - unit * jnp.mean(unit * grad_unit, axis=-1, keepdims=True))
    grad_all = lax.all_gather(grad_proj.astype(jnp.bfloat16), "dp", axis=0, tiled=True)
    grad_hidden = lax.dot_general(
        grad_all, w_second, (((1,), (1,)), ((), ())), preferred_element_type=jnp.float32
    )
    grad_pre = gelu_back(pre, grad_hidden).astype(jnp.bfloat16)
    sums = weight_sums(grad_all.T, gathered.T, hidden, grad_pre)
    return (sums[1], sums[0].T, grad_unit)


def solution(mesh):
    in_specs = (
        P(("dp", "group"), None),
        P(("dp", "group")),
        P("dp", None),
        P(None, "dp"),
        P("dp", None),
    )
    out_specs = (P("group", "dp"), P("dp", "group"), P(("dp", "group"), None))
    return jax.shard_map(
        per_device, mesh=mesh, in_specs=in_specs, out_specs=out_specs, check_vma=False
    )
```

```python
import functools

import jax
import jax.numpy as jnp
from jax import lax
from jax.experimental import pallas as pl
from jax.experimental.pallas import tpu as pltpu
from jax.sharding import PartitionSpec as P

EPS = 1e-06
TEMP = 10.0
SHIFT = -5.0
LEVELS = 32000.0
LANES = 128
CHUNK = 256
UNIT_PARTS = 4
VMEM_BYTES = 60 * 1024 * 1024
MESH = pl.DeviceIdType.MESH


def gelu_fwd(value):
    return jax.nn.gelu(value, approximate=True)


def gelu_back(pre, grad):
    _, back = jax.vjp(gelu_fwd, pre)
    return back(grad)[0]


def encode(value):
    flat = value.reshape(-1, value.shape[-1])
    top = jnp.max(jnp.abs(flat), axis=0, keepdims=True)
    joint = top[:, :LANES]
    for at in range(LANES, top.shape[1], LANES):
        joint = jnp.maximum(joint, top[:, at : at + LANES])
    joint = jnp.maximum(joint, 1e-30)
    inverse = jnp.tile(LEVELS / joint, (1, top.shape[1] // LANES))
    code = jnp.round(flat * inverse).astype(jnp.int32).astype(jnp.int16)
    return code.reshape(value.shape), jnp.broadcast_to(joint * (1.0 / LEVELS), (8, LANES))


def decode(code, scale):
    wide = jnp.tile(scale[0:1], (1, code.shape[-1] // LANES))
    return code.astype(jnp.int32).astype(jnp.float32) * wide


def weight_kernel(
    n_y,
    n_z,
    left0,
    left1,
    hidden,
    pre,
    grads,
    w_second,
    out,
    grad_pre,
    own,
    mine,
    y_out,
    y_in,
    y_scale_out,
    y_scale_in,
    z_out,
    z_in,
    z_scale_out,
    z_scale_in,
    y_sems,
    z_sems,
):
    me = lax.axis_index("group")
    z, y = me // n_y, me % n_y
    tall = out.shape[1]
    chunks = out.shape[2] // CHUNK

    def y_peer(d):
        return z * n_y + lax.rem(y + d, n_y)

    def z_peer(d):
        return lax.rem(z + d, n_z) * n_y + y

    def y_copies(i, d):
        return [
            pltpu.make_async_remote_copy(
                src_ref=a.at[i, d - 1],
                dst_ref=b.at[i, d - 1],
                send_sem=y_sems.at[which, 0, i, d - 1],
                recv_sem=y_sems.at[which, 1, i, d - 1],
                device_id={"group": y_peer(d)},
                device_id_type=MESH,
            )
            for which, (a, b) in enumerate(((y_out, y_in), (y_scale_out, y_scale_in)))
        ]

    def z_copies(i, d):
        return [
            pltpu.make_async_remote_copy(
                src_ref=a.at[i, d - 1],
                dst_ref=b.at[i, d - 1],
                send_sem=z_sems.at[which, 0, i, d - 1],
                recv_sem=z_sems.at[which, 1, i, d - 1],
                device_id={"group": z_peer(d)},
                device_id_type=MESH,
            )
            for which, (a, b) in enumerate(((z_out, z_in), (z_scale_out, z_scale_in)))
        ]

    barrier = pltpu.get_barrier_semaphore()
    for d in range(1, n_y):
        pl.semaphore_signal(barrier, inc=1, device_id={"group": y_peer(d)}, device_id_type=MESH)
    for d in range(1, n_z):
        pl.semaphore_signal(barrier, inc=1, device_id={"group": z_peer(d)}, device_id_type=MESH)
    pl.semaphore_wait(barrier, n_y + n_z - 2)

    def send_partials(i, left, rhs):
        def partial(owner_y, row):
            at = pl.multiple_of((row * n_y + owner_y) * tall, tall)
            return jnp.dot(left[pl.ds(at, tall), :], rhs, preferred_element_type=jnp.float32)

        for d in range(1, n_y):
            blocks = jnp.stack([partial(lax.rem(y + d, n_y), row) for row in range(n_z)])
            code, scale = encode(blocks)
            y_out[i, d - 1] = code
            y_scale_out[i, d - 1] = scale
            for copy in y_copies(i, d):
                copy.start()
        for row in range(n_z):
            own[i, row] = partial(y, row)

    def send_sums(i):
        for d in range(1, n_y):
            for copy in y_copies(i, d):
                copy.wait_recv()
        for d in range(1, n_z):
            row = lax.rem(z + d, n_z)
            block = own[i, row]
            for e in range(1, n_y):
                block = block + decode(y_in[i, e - 1, row], y_scale_in[i, e - 1])
            code, scale = encode(block)
            z_out[i, d - 1] = code
            z_scale_out[i, d - 1] = scale
            for copy in z_copies(i, d):
                copy.start()
        block = own[i, z]
        for e in range(1, n_y):
            block = block + decode(y_in[i, e - 1, z], y_scale_in[i, e - 1])
        mine[i] = block

    @pl.loop(0, chunks)
    def _(k):
        columns = pl.ds(pl.multiple_of(k * CHUNK, CHUNK), CHUNK)
        send_partials(k, left0, hidden[:, columns])

    @pl.loop(0, chunks)
    def _(k):
        columns = pl.ds(pl.multiple_of(k * CHUNK, CHUNK), CHUNK)
        w_rows = w_second[columns, :]

        @pl.loop(0, pre.shape[0] // CHUNK)
        def _(r):
            rows = pl.ds(pl.multiple_of(r * CHUNK, CHUNK), CHUNK)
            grad_hidden = lax.dot_general(
                grads[rows, :], w_rows, (((1,), (1,)), ((), ())), preferred_element_type=jnp.float32
            )
            grad_pre[rows, :] = gelu_back(pre[rows, columns], grad_hidden).astype(jnp.bfloat16)

        send_partials(chunks + k, left1, grad_pre[...])
        send_sums(k)

    @pl.loop(chunks, 2 * chunks)
    def _(i):
        send_sums(i)

    for m in range(2):

        @pl.loop(0, chunks)
        def _(k, m=m):
            i = m * chunks + k
            block = mine[i]
            for d in range(1, n_z):
                for copy in z_copies(i, d):
                    copy.wait_recv()
            for d in range(1, n_z):
                block = block + decode(z_in[i, d - 1], z_scale_in[i, d - 1])
            out[m, :, pl.ds(pl.multiple_of(k * CHUNK, CHUNK), CHUNK)] = block

    @pl.loop(0, 2 * chunks)
    def _(i):
        for d in range(1, n_y):
            for copy in y_copies(i, d):
                copy.wait_send()
        for d in range(1, n_z):
            for copy in z_copies(i, d):
                copy.wait_send()


def split(owners, shares):
    return shares // 2 if owners % (shares // 2) == 0 else 1


def weight_sums(left0, left1, hidden, pre, grads, w_second):
    owners, shares = lax.axis_size("group"), lax.axis_size("dp")
    n_y = split(owners, shares)
    n_z = owners // n_y
    tall = left0.shape[0] // owners
    wide = hidden.shape[1]
    items = 2 * (wide // CHUNK)
    vmem = pl.BlockSpec(memory_space=pltpu.VMEM)
    return pl.pallas_call(
        functools.partial(weight_kernel, n_y, n_z),
        out_shape=jax.ShapeDtypeStruct((2, tall, wide), jnp.float32),
        in_specs=[vmem] * 6,
        out_specs=vmem,
        scratch_shapes=[
            pltpu.VMEM((hidden.shape[0], CHUNK), jnp.bfloat16),
            pltpu.VMEM((items, n_z, tall, CHUNK), jnp.float32),
            pltpu.VMEM((items, tall, CHUNK), jnp.float32),
            pltpu.VMEM((items, n_y - 1, n_z, tall, CHUNK), jnp.int16),
            pltpu.VMEM((items, n_y - 1, n_z, tall, CHUNK), jnp.int16),
            pltpu.VMEM((items, n_y - 1, 8, LANES), jnp.float32),
            pltpu.VMEM((items, n_y - 1, 8, LANES), jnp.float32),
            pltpu.VMEM((items, n_z - 1, tall, CHUNK), jnp.int16),
            pltpu.VMEM((items, n_z - 1, tall, CHUNK), jnp.int16),
            pltpu.VMEM((items, n_z - 1, 8, LANES), jnp.float32),
            pltpu.VMEM((items, n_z - 1, 8, LANES), jnp.float32),
            pltpu.SemaphoreType.DMA((2, 2, items, n_y - 1)),
            pltpu.SemaphoreType.DMA((2, 2, items, n_z - 1)),
        ],
        compiler_params=pltpu.CompilerParams(
            collective_id=0, has_side_effects=True, vmem_limit_bytes=VMEM_BYTES
        ),
    )(left0, left1, hidden, pre, grads, w_second)


def front_kernel(
    n_x,
    n_y,
    n_z,
    embeds,
    ids_col,
    ids_row,
    times,
    w_first,
    w_second,
    gathered_t,
    pre,
    hidden,
    grad_unit,
    grads,
    grads_t,
    gathered,
    ids,
    units,
    unit,
    inverse,
    grad_all,
    core_out,
    core_in,
    x_out,
    x_in,
    kept,
    id_sems,
    gx_sems,
    gc_sems,
    pc_sems,
    px_sems,
    uz_sems,
    uy_sems,
):
    share, me = lax.axis_index("dp"), lax.axis_index("group")
    x, core = share // 2, share % 2
    z, y = me // n_y, me % n_y
    block, width = embeds.shape
    half = block // 2
    part = block // UNIT_PARTS
    n_g = n_y * n_z

    def remote(src, dst, sems, at, device):
        return pltpu.make_async_remote_copy(
            src_ref=src,
            dst_ref=dst,
            send_sem=sems.at[(0,) + at],
            recv_sem=sems.at[(1,) + at],
            device_id=device,
            device_id_type=MESH,
        )

    def share_at(dx, other):
        return lax.rem(x + n_x - dx, n_x) * 2 + (1 - core if other else core)

    def x_peer(d):
        return {"dp": lax.rem(x + d, n_x) * 2 + core}

    core_peer = {"dp": x * 2 + 1 - core}

    def owner_at(dz, dy):
        return lax.rem(z + n_z - dz, n_z) * n_y + lax.rem(y + n_y - dy, n_y)

    def z_peer(d):
        return {"group": lax.rem(z + d, n_z) * n_y + y}

    def y_peer(d):
        return {"group": z * n_y + lax.rem(y + d, n_y)}

    def g_peer(d):
        return {"group": lax.rem(me + d, n_g)}

    def rows(at, count):
        return pl.ds(pl.multiple_of(at, count), count)

    barrier = pltpu.get_barrier_semaphore()
    for d in range(1, n_x):
        pl.semaphore_signal(barrier, inc=1, device_id=x_peer(d), device_id_type=MESH)
    pl.semaphore_signal(barrier, inc=1, device_id=core_peer, device_id_type=MESH)
    for d in range(1, n_g):
        pl.semaphore_signal(barrier, inc=1, device_id=g_peer(d), device_id_type=MESH)
    pl.semaphore_wait(barrier, n_x - 1 + 1 + n_g - 1)

    def x_gather(buf, which, c, d):
        at = rows(share * block + c * half, half)
        return remote(buf.at[at], buf.at[at], gx_sems, (which, c, d - 1), x_peer(d))

    def core_gather(buf, which, c, d):
        at = rows(share_at(d, False) * block + c * half, half)
        return remote(buf.at[at], buf.at[at], gc_sems, (which, c, d), core_peer)

    gathered[rows(share * block, block), :] = embeds[...]
    for c in range(2):
        for d in range(1, n_x):
            x_gather(gathered, 0, c, d).start()
        core_gather(gathered, 0, c, 0).start()

    def id_copy(d):
        return remote(ids.at[me], ids.at[me], id_sems, (d - 1,), g_peer(d))

    ids[me] = ids_row[...]
    for d in range(1, n_g):
        id_copy(d).start()

    def product(j, c):
        at = rows(j * block + c * half, half)
        value = jnp.dot(gathered[at, :], w_first[...], preferred_element_type=jnp.float32)
        pre[at, :] = value
        value = gelu_fwd(value).astype(jnp.bfloat16)
        hidden[at, :] = value
        value = jnp.dot(value, w_second[...], preferred_element_type=jnp.float32)
        return value.astype(jnp.bfloat16)

    def core_sum(d, c):
        return remote(core_out.at[d, c], core_in.at[d, c], pc_sems, (d, c), core_peer)

    def x_sum(d, c):
        device = {"dp": share_at(d, False)}
        return remote(x_out.at[d - 1, c], x_in.at[d - 1, c], px_sems, (d - 1, c), device)

    for c in range(2):
        kept[rows(c * half, half), :] = product(share, c).astype(jnp.float32)
    for c in range(2):
        core_gather(gathered, 0, c, 0).wait_recv()
        core_out[0, c] = product(share_at(0, True), c)
        core_sum(0, c).start()
    for c in range(2):
        for d in range(1, n_x):
            x_gather(gathered, 0, c, d).wait_recv()
            core_gather(gathered, 0, c, d).start()
        for d in range(1, n_x):
            own = product(share_at(d, False), c).astype(jnp.float32)
            core_gather(gathered, 0, c, d).wait_recv()
            core_out[d, c] = product(share_at(d, True), c)
            core_sum(d, c).start()
            core_sum(d, c).wait_recv()
            own = own + core_in[d, c].astype(jnp.float32)
            x_out[d - 1, c] = own.astype(jnp.bfloat16)
            x_sum(d, c).start()

    def z_gather(p, d):
        at = rows(p * part, part)
        return remote(units.at[me, at], units.at[me, at], uz_sems, (p, d - 1), z_peer(d))

    def y_gather(p, dz, d):
        b, at = owner_at(dz, 0), rows(p * part, part)
        return remote(units.at[b, at], units.at[b, at], uy_sems, (p, dz, d - 1), y_peer(d))

    for c in range(2):
        at = rows(c * half, half)
        core_sum(0, c).wait_recv()
        proj = kept[at, :] + core_in[0, c].astype(jnp.float32)
        for d in range(1, n_x):
            x_sum(d, c).wait_recv()
            proj = proj + x_in[d - 1, c].astype(jnp.float32)
        inv = lax.rsqrt(jnp.mean(proj * proj, axis=-1, keepdims=True) + EPS)
        value = proj * inv
        inverse[at, :] = jnp.broadcast_to(inv, (half, LANES))
        unit[at, :] = value
        units[me, at, :] = value.astype(jnp.bfloat16)
        for p in range(c * UNIT_PARTS // 2, (c + 1) * UNIT_PARTS // 2):
            for d in range(1, n_z):
                z_gather(p, d).start()
            for d in range(1, n_y):
                y_gather(p, 0, d).start()

    for d in range(1, n_g):
        id_copy(d).wait_recv()
    grad_unit[...] = jnp.zeros(grad_unit.shape, jnp.float32)

    def add_block(b):
        logits = (
            TEMP
            / width_of(units)
            * lax.dot_general(
                units[me], units[b], (((1,), (1,)), ((), ())), preferred_element_type=jnp.float32
            )
            + SHIFT
        )
        sign = jnp.where(ids_col[...] == ids[b][0:1, :], 1.0, -1.0).astype(jnp.float32)
        weight = (-sign * jax.nn.sigmoid(-sign * logits) * (TEMP / width_of(units))).astype(
            jnp.bfloat16
        )
        weight = (weight.astype(jnp.float32) * times[b][0:1, 0:1]).astype(jnp.bfloat16)
        grad_unit[...] += jnp.dot(weight, units[b], preferred_element_type=jnp.float32)

    add_block(me)

    @pl.loop(0, n_x * 2)
    def _(j):
        at = rows(j * block, block)
        gathered_t[:, at] = gathered[at, :].T

    for p in range(UNIT_PARTS):
        for dz in range(1, n_z):
            z_gather(p, dz).wait_recv()
            for d in range(1, n_y):
                y_gather(p, dz, d).start()

    @pl.loop(1, n_z)
    def _(dz):
        add_block(owner_at(dz, 0))

    for dy in range(1, n_y):
        for p in range(UNIT_PARTS):
            y_gather(p, 0, dy).wait_recv()
        add_block(owner_at(0, dy))

        @pl.loop(1, n_z)
        def _(dz, dy=dy):
            for p in range(UNIT_PARTS):
                y_gather(p, dz, dy).wait_recv()
            add_block(owner_at(dz, dy))

    for c in range(2):
        at = rows(c * half, half)
        total, value = grad_unit[at, :], unit[at, :]
        slope = jnp.mean(value * total, axis=-1, keepdims=True)
        grad = inverse[at, 0:1] * (total - value * slope)
        grad_all[rows(share * block + c * half, half), :] = grad.astype(jnp.bfloat16)
        for d in range(1, n_x):
            x_gather(grad_all, 1, c, d).start()
        core_gather(grad_all, 1, c, 0).start()

    def hand_out(j):
        at = rows(j * block, block)
        value = grad_all[at, :]
        grads[at, :] = value
        grads_t[:, at] = value.T

    hand_out(share)
    for c in range(2):
        for d in range(1, n_x):
            x_gather(grad_all, 1, c, d).wait_recv()
            core_gather(grad_all, 1, c, d).start()
    for d in range(n_x):
        if d > 0:
            hand_out(share_at(d, False))
        for c in range(2):
            core_gather(grad_all, 1, c, d).wait_recv()
        hand_out(share_at(d, True))

    for d in range(1, n_g):
        id_copy(d).wait_send()
    for c in range(2):
        for which, buf in enumerate((gathered, grad_all)):
            for d in range(1, n_x):
                x_gather(buf, which, c, d).wait_send()
            for d in range(n_x):
                core_gather(buf, which, c, d).wait_send()
        for d in range(n_x):
            core_sum(d, c).wait_send()
        for d in range(1, n_x):
            x_sum(d, c).wait_send()

    for p in range(UNIT_PARTS):
        for d in range(1, n_z):
            z_gather(p, d).wait_send()
        for d in range(1, n_y):
            for dz in range(n_z):
                y_gather(p, dz, d).wait_send()


def width_of(units):
    return units.shape[-1]


def front(embeds, row_ids, times, w_first, w_second):
    owners, shares = lax.axis_size("group"), lax.axis_size("dp")
    n_y = split(owners, shares)
    n_z, n_x = owners // n_y, shares // 2
    block, wide = embeds.shape
    total, hid, width = shares * block, w_second.shape[0], w_second.shape[1]
    half = block // 2
    vmem = pl.BlockSpec(memory_space=pltpu.VMEM)
    dma = pltpu.SemaphoreType.DMA
    bf16, f32 = jnp.bfloat16, jnp.float32
    return pl.pallas_call(
        functools.partial(front_kernel, n_x, n_y, n_z),
        out_shape=[
            jax.ShapeDtypeStruct((wide, total), bf16),
            jax.ShapeDtypeStruct((total, hid), f32),
            jax.ShapeDtypeStruct((total, hid), bf16),
            jax.ShapeDtypeStruct((block, width), f32),
            jax.ShapeDtypeStruct((total, width), bf16),
            jax.ShapeDtypeStruct((width, total), bf16),
        ],
        in_specs=[vmem] * 6,
        out_specs=[vmem] * 6,
        scratch_shapes=[
            pltpu.VMEM((total, wide), bf16),
            pltpu.VMEM((owners, 8, block), jnp.int32),
            pltpu.VMEM((owners, block, width), bf16),
            pltpu.VMEM((block, width), f32),
            pltpu.VMEM((block, LANES), f32),
            pltpu.VMEM((total, width), bf16),
            pltpu.VMEM((n_x, 2, half, width), bf16),
            pltpu.VMEM((n_x, 2, half, width), bf16),
            pltpu.VMEM((n_x - 1, 2, half, width), bf16),
            pltpu.VMEM((n_x - 1, 2, half, width), bf16),
            pltpu.VMEM((block, width), f32),
            dma((2, owners - 1)),
            dma((2, 2, 2, n_x - 1)),
            dma((2, 2, 2, n_x)),
            dma((2, n_x, 2)),
            dma((2, n_x - 1, 2)),
            dma((2, UNIT_PARTS, n_z - 1)),
            dma((2, UNIT_PARTS, n_z, n_y - 1)),
        ],
        compiler_params=pltpu.CompilerParams(
            collective_id=1, has_side_effects=True, vmem_limit_bytes=VMEM_BYTES
        ),
    )(
        embeds,
        row_ids[:, None],
        jnp.broadcast_to(row_ids[None, :], (8, block)),
        jnp.broadcast_to(times[:, None, None], (owners, 8, LANES)),
        w_first,
        w_second,
    )


def per_device(embeds, row_ids, neighbors, w_first, w_second):
    owners = lax.axis_size("group")
    me = lax.axis_index("group")
    others = jnp.arange(owners, dtype=jnp.int32)
    mine = lax.dynamic_index_in_dim(neighbors, me, 0, keepdims=False)
    lists = jnp.sum((mine[None, :] == others[:, None]).astype(jnp.float32), axis=1)
    listed_by = jnp.sum((neighbors == me).astype(jnp.float32), axis=1)
    times = jnp.where(others == me, 2.0, lists + listed_by)
    gathered_t, pre, hidden, grad_unit, grads, grads_t = front(
        embeds, row_ids, times, w_first, w_second
    )
    sums = weight_sums(grads_t, gathered_t, hidden, pre, grads, w_second)
    return (sums[1], sums[0].T, grad_unit)


def solution(mesh):
    in_specs = (
        P(("dp", "group"), None),
        P(("dp", "group")),
        P("dp", None),
        P(None, "dp"),
        P("dp", None),
    )
    out_specs = (P("group", "dp"), P("dp", "group"), P(("dp", "group"), None))
    return jax.shard_map(
        per_device, mesh=mesh, in_specs=in_specs, out_specs=out_specs, check_vma=False
    )
```

```python
import functools

import jax
import jax.numpy as jnp
from jax import lax
from jax.experimental import pallas as pl
from jax.experimental.pallas import tpu as pltpu
from jax.sharding import PartitionSpec as P

EPS = 1e-06
TEMP = 10.0
SHIFT = -5.0
LEVELS = 32000.0
LANES = 128
CHUNK = 256
UNIT_PARTS = 4
VMEM_BYTES = 63 * 1024 * 1024
MESH = pl.DeviceIdType.MESH


def gelu_fwd(value):
    return jax.nn.gelu(value, approximate=True)


def gelu_back(pre, grad):
    _, back = jax.vjp(gelu_fwd, pre)
    return back(grad)[0]


def encode(value):
    flat = value.reshape(-1, value.shape[-1])
    top = jnp.max(jnp.abs(flat), axis=0, keepdims=True)
    joint = top[:, :LANES]
    for at in range(LANES, top.shape[1], LANES):
        joint = jnp.maximum(joint, top[:, at : at + LANES])
    joint = jnp.maximum(joint, 1e-30)
    inverse = jnp.tile(LEVELS / joint, (1, top.shape[1] // LANES))
    code = jnp.round(flat * inverse).astype(jnp.int32).astype(jnp.int16)
    return code.reshape(value.shape), jnp.broadcast_to(joint * (1.0 / LEVELS), (8, LANES))


def decode(code, scale):
    wide = jnp.tile(scale[0:1], (1, code.shape[-1] // LANES))
    return code.astype(jnp.int32).astype(jnp.float32) * wide


def weight_part(
    n_y,
    n_z,
    left0,
    left1,
    hidden,
    pre,
    grads,
    w_second,
    first,
    second,
    grad_pre,
    own,
    mine,
    y_out,
    y_in,
    y_scale_out,
    y_scale_in,
    z_out,
    z_in,
    z_scale_out,
    z_scale_in,
    y_sems,
    z_sems,
):
    me = lax.axis_index("group")
    z, y = me // n_y, me % n_y
    tall = first.shape[0]
    chunks = first.shape[1] // CHUNK

    def y_peer(d):
        return z * n_y + lax.rem(y + d, n_y)

    def z_peer(d):
        return lax.rem(z + d, n_z) * n_y + y

    def y_copies(i, d):
        return [
            pltpu.make_async_remote_copy(
                src_ref=a.at[i, d - 1],
                dst_ref=b.at[i, d - 1],
                send_sem=y_sems.at[which, 0, i, d - 1],
                recv_sem=y_sems.at[which, 1, i, d - 1],
                device_id={"group": y_peer(d)},
                device_id_type=MESH,
            )
            for which, (a, b) in enumerate(((y_out, y_in), (y_scale_out, y_scale_in)))
        ]

    def z_copies(i, d):
        return [
            pltpu.make_async_remote_copy(
                src_ref=a.at[i, d - 1],
                dst_ref=b.at[i, d - 1],
                send_sem=z_sems.at[which, 0, i, d - 1],
                recv_sem=z_sems.at[which, 1, i, d - 1],
                device_id={"group": z_peer(d)},
                device_id_type=MESH,
            )
            for which, (a, b) in enumerate(((z_out, z_in), (z_scale_out, z_scale_in)))
        ]

    def send_partials(i, left, rhs):
        def partial(owner_y, row):
            at = pl.multiple_of((row * n_y + owner_y) * tall, tall)
            return jnp.dot(left[pl.ds(at, tall), :], rhs, preferred_element_type=jnp.float32)

        for d in range(1, n_y):
            blocks = jnp.stack([partial(lax.rem(y + d, n_y), row) for row in range(n_z)])
            code, scale = encode(blocks)
            y_out[i, d - 1] = code
            y_scale_out[i, d - 1] = scale
            for copy in y_copies(i, d):
                copy.start()
        for row in range(n_z):
            own[i, row] = partial(y, row)

    def send_sums(i):
        for d in range(1, n_y):
            for copy in y_copies(i, d):
                copy.wait_recv()
        for d in range(1, n_z):
            row = lax.rem(z + d, n_z)
            block = own[i, row]
            for e in range(1, n_y):
                block = block + decode(y_in[i, e - 1, row], y_scale_in[i, e - 1])
            code, scale = encode(block)
            z_out[i, d - 1] = code
            z_scale_out[i, d - 1] = scale
            for copy in z_copies(i, d):
                copy.start()
        block = own[i, z]
        for e in range(1, n_y):
            block = block + decode(y_in[i, e - 1, z], y_scale_in[i, e - 1])
        mine[i] = block

    @pl.loop(0, chunks)
    def _(k):
        columns = pl.ds(pl.multiple_of(k * CHUNK, CHUNK), CHUNK)
        send_partials(k, left0, hidden[:, columns])

    @pl.loop(0, chunks)
    def _(k):
        columns = pl.ds(pl.multiple_of(k * CHUNK, CHUNK), CHUNK)
        w_rows = w_second[columns, :]

        @pl.loop(0, pre.shape[0] // CHUNK)
        def _(r):
            rows = pl.ds(pl.multiple_of(r * CHUNK, CHUNK), CHUNK)
            grad_hidden = lax.dot_general(
                grads[rows, :], w_rows, (((1,), (1,)), ((), ())), preferred_element_type=jnp.float32
            )
            grad_pre[rows, :] = gelu_back(pre[rows, columns], grad_hidden).astype(jnp.bfloat16)

        send_partials(chunks + k, left1, grad_pre[...])
        send_sums(k)

    @pl.loop(chunks, 2 * chunks)
    def _(i):
        send_sums(i)

    for m in range(2):

        @pl.loop(0, chunks)
        def _(k, m=m):
            i = m * chunks + k
            block = mine[i]
            for d in range(1, n_z):
                for copy in z_copies(i, d):
                    copy.wait_recv()
            for d in range(1, n_z):
                block = block + decode(z_in[i, d - 1], z_scale_in[i, d - 1])
            at = pl.ds(pl.multiple_of(k * CHUNK, CHUNK), CHUNK)
            if m == 0:
                second[at, :] = block.T
            else:
                first[:, at] = block

    @pl.loop(0, 2 * chunks)
    def _(i):
        for d in range(1, n_y):
            for copy in y_copies(i, d):
                copy.wait_send()
        for d in range(1, n_z):
            for copy in z_copies(i, d):
                copy.wait_send()


def split(owners, shares):
    return shares // 2 if owners % (shares // 2) == 0 else 1


def step_kernel(
    n_x,
    n_y,
    n_z,
    embeds,
    own_ids,
    neighbors,
    w_first,
    w_second,
    first,
    second,
    grad_unit,
    gathered_t,
    pre,
    hidden,
    grads_t,
    ids_col,
    gathered,
    ids,
    units,
    unit,
    inverse,
    grad_all,
    core_out,
    core_in,
    x_out,
    x_in,
    id_sems,
    gx_sems,
    gc_sems,
    pc_sems,
    px_sems,
    uz_sems,
    uy_sems,
    *weight_scratch,
):
    share, me = lax.axis_index("dp"), lax.axis_index("group")
    x, core = share // 2, share % 2
    z, y = me // n_y, me % n_y
    block, width = embeds.shape
    half = block // 2
    part = block // UNIT_PARTS
    n_g = n_y * n_z

    def remote(src, dst, sems, at, device):
        return pltpu.make_async_remote_copy(
            src_ref=src,
            dst_ref=dst,
            send_sem=sems.at[(0,) + at],
            recv_sem=sems.at[(1,) + at],
            device_id=device,
            device_id_type=MESH,
        )

    def share_at(dx, other):
        return lax.rem(x + n_x - dx, n_x) * 2 + (1 - core if other else core)

    def x_peer(d):
        return {"dp": lax.rem(x + d, n_x) * 2 + core}

    core_peer = {"dp": x * 2 + 1 - core}

    def owner_at(dz, dy):
        return lax.rem(z + n_z - dz, n_z) * n_y + lax.rem(y + n_y - dy, n_y)

    def z_peer(d):
        return {"group": lax.rem(z + d, n_z) * n_y + y}

    def y_peer(d):
        return {"group": z * n_y + lax.rem(y + d, n_y)}

    def g_peer(d):
        return {"group": lax.rem(me + d, n_g)}

    def rows(at, count):
        return pl.ds(pl.multiple_of(at, count), count)

    barrier = pltpu.get_barrier_semaphore()
    for d in range(1, n_x):
        pl.semaphore_signal(barrier, inc=1, device_id=x_peer(d), device_id_type=MESH)
    pl.semaphore_signal(barrier, inc=1, device_id=core_peer, device_id_type=MESH)
    for d in range(1, n_g):
        pl.semaphore_signal(barrier, inc=1, device_id=g_peer(d), device_id_type=MESH)
    pl.semaphore_wait(barrier, n_x - 1 + 1 + n_g - 1)

    def x_gather(buf, which, c, d):
        at = rows(share * block + c * half, half)
        return remote(buf.at[at], buf.at[at], gx_sems, (which, c, d - 1), x_peer(d))

    def core_gather(buf, which, c, d):
        at = rows(share_at(d, False) * block + c * half, half)
        return remote(buf.at[at], buf.at[at], gc_sems, (which, c, d), core_peer)

    gathered[rows(share * block, block), :] = embeds[...]
    for c in range(2):
        for d in range(1, n_x):
            x_gather(gathered, 0, c, d).start()
        core_gather(gathered, 0, c, 0).start()

    def id_copy(d):
        return remote(ids.at[me], ids.at[me], id_sems, (d - 1,), g_peer(d))

    ids[me] = jnp.broadcast_to(own_ids[...], ids.shape[1:])
    for d in range(1, n_g):
        id_copy(d).start()

    def product(j, c, count):
        at = rows(j * block + c * half, count)
        value = jnp.dot(gathered[at, :], w_first[...], preferred_element_type=jnp.float32)
        pre[at, :] = value
        value = gelu_fwd(value).astype(jnp.bfloat16)
        hidden[at, :] = value
        value = jnp.dot(value, w_second[...], preferred_element_type=jnp.float32)
        return value.astype(jnp.bfloat16)

    def core_sum(d, c):
        return remote(core_out.at[d, c], core_in.at[d, c], pc_sems, (d, c), core_peer)

    def x_sum(d, c):
        device = {"dp": share_at(d, False)}
        return remote(x_out.at[d - 1, c], x_in.at[d - 1, c], px_sems, (d - 1, c), device)

    unit[...] = product(share, 0, block).astype(jnp.float32)
    for c in range(2):
        core_gather(gathered, 0, c, 0).wait_recv()
    core_out[0] = product(share_at(0, True), 0, block).reshape(core_out.shape[1:])
    for c in range(2):
        core_sum(0, c).start()
    for c in range(2):
        for d in range(1, n_x):
            x_gather(gathered, 0, c, d).wait_recv()
            core_gather(gathered, 0, c, d).start()
        for d in range(1, n_x):
            own = product(share_at(d, False), c, half).astype(jnp.float32)
            core_gather(gathered, 0, c, d).wait_recv()
            core_out[d, c] = product(share_at(d, True), c, half)
            core_sum(d, c).start()
            core_sum(d, c).wait_recv()
            own = own + core_in[d, c].astype(jnp.float32)
            x_out[d - 1, c] = own.astype(jnp.bfloat16)
            x_sum(d, c).start()

    def z_gather(p, d):
        at = rows(p * part, part)
        return remote(units.at[me, at], units.at[me, at], uz_sems, (p, d - 1), z_peer(d))

    def y_gather(p, dz, d):
        b, at = owner_at(dz, 0), rows(p * part, part)
        return remote(units.at[b, at], units.at[b, at], uy_sems, (p, dz, d - 1), y_peer(d))

    for c in range(2):
        at = rows(c * half, half)
        core_sum(0, c).wait_recv()
        proj = unit[at, :] + core_in[0, c].astype(jnp.float32)
        for d in range(1, n_x):
            x_sum(d, c).wait_recv()
            proj = proj + x_in[d - 1, c].astype(jnp.float32)
        inv = lax.rsqrt(jnp.mean(proj * proj, axis=-1, keepdims=True) + EPS)
        value = proj * inv
        inverse[at, :] = jnp.broadcast_to(inv, (half, LANES))
        unit[at, :] = value
        units[me, at, :] = value.astype(jnp.bfloat16)
        for p in range(c * UNIT_PARTS // 2, (c + 1) * UNIT_PARTS // 2):
            for d in range(1, n_z):
                z_gather(p, d).start()
            for d in range(1, n_y):
                y_gather(p, 0, d).start()

    for d in range(1, n_g):
        id_copy(d).wait_recv()
    grad_unit[...] = jnp.zeros(grad_unit.shape, jnp.float32)
    ids_col[...] = ids[me].T

    def add_block(b):
        logits = (
            TEMP
            / width_of(units)
            * lax.dot_general(
                units[me], units[b], (((1,), (1,)), ((), ())), preferred_element_type=jnp.float32
            )
            + SHIFT
        )
        sign = jnp.where(ids_col[:, 0:1] == ids[b][0:1, :], 1.0, -1.0).astype(jnp.float32)
        weight = (-sign * jax.nn.sigmoid(-sign * logits) * (TEMP / width_of(units))).astype(
            jnp.bfloat16
        )
        lists = (neighbors[pl.ds(me, 1), :] == b).astype(jnp.float32)
        listed_by = (neighbors[pl.ds(b, 1), :] == me).astype(jnp.float32)
        times = jnp.sum(lists + listed_by, axis=1, keepdims=True)
        times = jnp.where(b == me, 2.0, times)
        weight = (weight.astype(jnp.float32) * times).astype(jnp.bfloat16)
        grad_unit[...] += jnp.dot(weight, units[b], preferred_element_type=jnp.float32)

    add_block(me)

    @pl.loop(0, n_x * 2)
    def _(j):
        at = rows(j * block, block)
        gathered_t[:, at] = gathered[at, :].T

    for p in range(UNIT_PARTS):
        for dz in range(1, n_z):
            z_gather(p, dz).wait_recv()
            for d in range(1, n_y):
                y_gather(p, dz, d).start()

    @pl.loop(1, n_z)
    def _(dz):
        add_block(owner_at(dz, 0))

    for dy in range(1, n_y):
        for p in range(UNIT_PARTS):
            y_gather(p, 0, dy).wait_recv()
        add_block(owner_at(0, dy))

        @pl.loop(1, n_z)
        def _(dz, dy=dy):
            for p in range(UNIT_PARTS):
                y_gather(p, dz, dy).wait_recv()
            add_block(owner_at(dz, dy))

    for c in range(2):
        at = rows(c * half, half)
        total, value = grad_unit[at, :], unit[at, :]
        slope = jnp.mean(value * total, axis=-1, keepdims=True)
        grad = inverse[at, 0:1] * (total - value * slope)
        grad_all[rows(share * block + c * half, half), :] = grad.astype(jnp.bfloat16)
        for d in range(1, n_x):
            x_gather(grad_all, 1, c, d).start()
        core_gather(grad_all, 1, c, 0).start()

    def hand_out(j):
        at = rows(j * block, block)
        grads_t[:, at] = grad_all[at, :].T

    hand_out(share)
    for c in range(2):
        for d in range(1, n_x):
            x_gather(grad_all, 1, c, d).wait_recv()
            core_gather(grad_all, 1, c, d).start()
    for d in range(n_x):
        if d > 0:
            hand_out(share_at(d, False))
        for c in range(2):
            core_gather(grad_all, 1, c, d).wait_recv()
        hand_out(share_at(d, True))

    weight_part(
        n_y,
        n_z,
        grads_t,
        gathered_t,
        hidden,
        pre,
        grad_all,
        w_second,
        first,
        second,
        *weight_scratch,
    )

    for d in range(1, n_g):
        id_copy(d).wait_send()
    for c in range(2):
        for which, buf in enumerate((gathered, grad_all)):
            for d in range(1, n_x):
                x_gather(buf, which, c, d).wait_send()
            for d in range(n_x):
                core_gather(buf, which, c, d).wait_send()
        for d in range(n_x):
            core_sum(d, c).wait_send()
        for d in range(1, n_x):
            x_sum(d, c).wait_send()

    for p in range(UNIT_PARTS):
        for d in range(1, n_z):
            z_gather(p, d).wait_send()
        for d in range(1, n_y):
            for dz in range(n_z):
                y_gather(p, dz, d).wait_send()


def width_of(units):
    return units.shape[-1]


def step(embeds, row_ids, neighbors, w_first, w_second):
    owners, shares = lax.axis_size("group"), lax.axis_size("dp")
    n_y = split(owners, shares)
    n_z, n_x = owners // n_y, shares // 2
    block, wide = embeds.shape
    total, hid, width = shares * block, w_second.shape[0], w_second.shape[1]
    half, tall = block // 2, wide // owners
    items = 2 * (hid // CHUNK)
    vmem = pl.BlockSpec(memory_space=pltpu.VMEM)
    dma = pltpu.SemaphoreType.DMA
    bf16, f32, i16 = jnp.bfloat16, jnp.float32, jnp.int16
    return pl.pallas_call(
        functools.partial(step_kernel, n_x, n_y, n_z),
        out_shape=[
            jax.ShapeDtypeStruct((tall, hid), f32),
            jax.ShapeDtypeStruct((hid, tall), f32),
            jax.ShapeDtypeStruct((block, width), f32),
        ],
        in_specs=[vmem] * 5,
        out_specs=[vmem] * 3,
        scratch_shapes=[
            pltpu.VMEM((wide, total), bf16),
            pltpu.VMEM((total, hid), f32),
            pltpu.VMEM((total, hid), bf16),
            pltpu.VMEM((width, total), bf16),
            pltpu.VMEM((block, 8), jnp.int32),
            pltpu.VMEM((total, wide), bf16),
            pltpu.VMEM((owners, 8, block), jnp.int32),
            pltpu.VMEM((owners, block, width), bf16),
            pltpu.VMEM((block, width), f32),
            pltpu.VMEM((block, LANES), f32),
            pltpu.VMEM((total, width), bf16),
            pltpu.VMEM((n_x, 2, half, width), bf16),
            pltpu.VMEM((n_x, 2, half, width), bf16),
            pltpu.VMEM((n_x - 1, 2, half, width), bf16),
            pltpu.VMEM((n_x - 1, 2, half, width), bf16),
            dma((2, owners - 1)),
            dma((2, 2, 2, n_x - 1)),
            dma((2, 2, 2, n_x)),
            dma((2, n_x, 2)),
            dma((2, n_x - 1, 2)),
            dma((2, UNIT_PARTS, n_z - 1)),
            dma((2, UNIT_PARTS, n_z, n_y - 1)),
            pltpu.VMEM((total, CHUNK), bf16),
            pltpu.VMEM((items, n_z, tall, CHUNK), f32),
            pltpu.VMEM((items, tall, CHUNK), f32),
            pltpu.VMEM((items, n_y - 1, n_z, tall, CHUNK), i16),
            pltpu.VMEM((items, n_y - 1, n_z, tall, CHUNK), i16),
            pltpu.VMEM((items, n_y - 1, 8, LANES), f32),
            pltpu.VMEM((items, n_y - 1, 8, LANES), f32),
            pltpu.VMEM((items, n_z - 1, tall, CHUNK), i16),
            pltpu.VMEM((items, n_z - 1, tall, CHUNK), i16),
            pltpu.VMEM((items, n_z - 1, 8, LANES), f32),
            pltpu.VMEM((items, n_z - 1, 8, LANES), f32),
            dma((2, 2, items, n_y - 1)),
            dma((2, 2, items, n_z - 1)),
        ],
        compiler_params=pltpu.CompilerParams(
            collective_id=0, has_side_effects=True, vmem_limit_bytes=VMEM_BYTES
        ),
    )(embeds, row_ids[None, :], neighbors, w_first, w_second)


def per_device(embeds, row_ids, neighbors, w_first, w_second):
    return tuple(step(embeds, row_ids, neighbors, w_first, w_second))


def solution(mesh):
    in_specs = (
        P(("dp", "group"), None),
        P(("dp", "group")),
        P("dp", None),
        P(None, "dp"),
        P("dp", None),
    )
    out_specs = (P("group", "dp"), P("dp", "group"), P(("dp", "group"), None))
    return jax.shard_map(
        per_device, mesh=mesh, in_specs=in_specs, out_specs=out_specs, check_vma=False
    )
```

```python
import functools

import jax
import jax.numpy as jnp
from jax import lax
from jax.experimental import pallas as pl
from jax.experimental.pallas import tpu as pltpu
from jax.sharding import PartitionSpec as P

EPS = 1e-06
TEMP = 10.0
SHIFT = -5.0
LEVELS = 32000.0
LANES = 128
CHUNK = 256
PARTS = 4
VMEM_BYTES = 63 * 1024 * 1024
MESH = pl.DeviceIdType.MESH


def gelu_fwd(value):
    return jax.nn.gelu(value, approximate=True)


def gelu_back(pre, grad):
    _, back = jax.vjp(gelu_fwd, pre)
    return back(grad)[0]


def encode(value):
    flat = value.reshape(-1, value.shape[-1])
    top = jnp.max(jnp.abs(flat), axis=0, keepdims=True)
    joint = top[:, :LANES]
    for at in range(LANES, top.shape[1], LANES):
        joint = jnp.maximum(joint, top[:, at : at + LANES])
    joint = jnp.maximum(joint, 1e-30)
    inverse = jnp.tile(LEVELS / joint, (1, top.shape[1] // LANES))
    code = jnp.round(flat * inverse).astype(jnp.int32).astype(jnp.int16)
    return code.reshape(value.shape), jnp.broadcast_to(joint * (1.0 / LEVELS), (8, LANES))


def decode(code, scale):
    wide = jnp.tile(scale[0:1], (1, code.shape[-1] // LANES))
    return code.astype(jnp.int32).astype(jnp.float32) * wide


def weight_part(
    n_y,
    n_z,
    left0,
    left1,
    hidden,
    pre,
    grads,
    w_second,
    first,
    second,
    grad_pre,
    own,
    mine,
    y_out,
    y_in,
    y_scale_out,
    y_scale_in,
    z_out,
    z_in,
    z_scale_out,
    z_scale_in,
    y_sems,
    z_sems,
):
    me = lax.axis_index("group")
    z, y = me // n_y, me % n_y
    tall = first.shape[0]
    chunks = first.shape[1] // CHUNK

    def y_peer(d):
        return z * n_y + lax.rem(y + d, n_y)

    def z_peer(d):
        return lax.rem(z + d, n_z) * n_y + y

    def y_copies(i, d):
        return [
            pltpu.make_async_remote_copy(
                src_ref=a.at[i, d - 1],
                dst_ref=b.at[i, d - 1],
                send_sem=y_sems.at[which, 0, i, d - 1],
                recv_sem=y_sems.at[which, 1, i, d - 1],
                device_id={"group": y_peer(d)},
                device_id_type=MESH,
            )
            for which, (a, b) in enumerate(((y_out, y_in), (y_scale_out, y_scale_in)))
        ]

    def z_copies(i, d):
        return [
            pltpu.make_async_remote_copy(
                src_ref=a.at[i, d - 1],
                dst_ref=b.at[i, d - 1],
                send_sem=z_sems.at[which, 0, i, d - 1],
                recv_sem=z_sems.at[which, 1, i, d - 1],
                device_id={"group": z_peer(d)},
                device_id_type=MESH,
            )
            for which, (a, b) in enumerate(((z_out, z_in), (z_scale_out, z_scale_in)))
        ]

    def send_partials(i, left, rhs):
        def partial(owner_y, row):
            at = pl.multiple_of((row * n_y + owner_y) * tall, tall)
            return jnp.dot(left[pl.ds(at, tall), :], rhs, preferred_element_type=jnp.float32)

        for d in range(1, n_y):
            blocks = jnp.stack([partial(lax.rem(y + d, n_y), row) for row in range(n_z)])
            code, scale = encode(blocks)
            y_out[i, d - 1] = code
            y_scale_out[i, d - 1] = scale
            for copy in y_copies(i, d):
                copy.start()
        for row in range(n_z):
            own[i, row] = partial(y, row)

    def send_sums(i):
        for d in range(1, n_y):
            for copy in y_copies(i, d):
                copy.wait_recv()
        for d in range(1, n_z):
            row = lax.rem(z + d, n_z)
            block = own[i, row]
            for e in range(1, n_y):
                block = block + decode(y_in[i, e - 1, row], y_scale_in[i, e - 1])
            code, scale = encode(block)
            z_out[i, d - 1] = code
            z_scale_out[i, d - 1] = scale
            for copy in z_copies(i, d):
                copy.start()
        block = own[i, z]
        for e in range(1, n_y):
            block = block + decode(y_in[i, e - 1, z], y_scale_in[i, e - 1])
        mine[i] = block

    @pl.loop(0, chunks)
    def _(k):
        columns = pl.ds(pl.multiple_of(k * CHUNK, CHUNK), CHUNK)
        send_partials(k, left0, hidden[:, columns])

    @pl.loop(0, chunks)
    def _(k):
        columns = pl.ds(pl.multiple_of(k * CHUNK, CHUNK), CHUNK)
        w_rows = w_second[columns, :]

        @pl.loop(0, pre.shape[0] // CHUNK)
        def _(r):
            rows = pl.ds(pl.multiple_of(r * CHUNK, CHUNK), CHUNK)
            grad_hidden = lax.dot_general(
                grads[rows, :], w_rows, (((1,), (1,)), ((), ())), preferred_element_type=jnp.float32
            )
            grad_pre[rows, :] = gelu_back(pre[rows, columns], grad_hidden).astype(jnp.bfloat16)

        send_partials(chunks + k, left1, grad_pre[...])
        send_sums(k)

    @pl.loop(chunks, 2 * chunks)
    def _(i):
        send_sums(i)

    for m in range(2):

        @pl.loop(0, chunks)
        def _(k, m=m):
            i = m * chunks + k
            block = mine[i]
            for d in range(1, n_z):
                for copy in z_copies(i, d):
                    copy.wait_recv()
            for d in range(1, n_z):
                block = block + decode(z_in[i, d - 1], z_scale_in[i, d - 1])
            at = pl.ds(pl.multiple_of(k * CHUNK, CHUNK), CHUNK)
            if m == 0:
                second[at, :] = block.T
            else:
                first[:, at] = block

    @pl.loop(0, 2 * chunks)
    def _(i):
        for d in range(1, n_y):
            for copy in y_copies(i, d):
                copy.wait_send()
        for d in range(1, n_z):
            for copy in z_copies(i, d):
                copy.wait_send()


def split(owners, shares):
    return shares // 2 if owners % (shares // 2) == 0 else 1


def step_kernel(
    n_x,
    n_y,
    n_z,
    embeds,
    own_ids,
    neighbors,
    w_first,
    w_second,
    first,
    second,
    grad_unit,
    gathered_t,
    pre,
    hidden,
    grads_t,
    ids_col,
    gathered,
    ids,
    units,
    unit,
    inverse,
    grad_all,
    core_out,
    core_in,
    x_out,
    x_in,
    id_sems,
    gx_sems,
    gc_sems,
    pc_sems,
    px_sems,
    uz_sems,
    uy_sems,
    *weight_scratch,
):
    share, me = lax.axis_index("dp"), lax.axis_index("group")
    x, core = share // 2, share % 2
    z, y = me // n_y, me % n_y
    block, width = embeds.shape
    part = block // PARTS
    n_g = n_y * n_z

    def remote(src, dst, sems, at, device):
        return pltpu.make_async_remote_copy(
            src_ref=src,
            dst_ref=dst,
            send_sem=sems.at[(0,) + at],
            recv_sem=sems.at[(1,) + at],
            device_id=device,
            device_id_type=MESH,
        )

    def share_at(dx, other):
        return lax.rem(x + n_x - dx, n_x) * 2 + (1 - core if other else core)

    def x_peer(d):
        return {"dp": lax.rem(x + d, n_x) * 2 + core}

    core_peer = {"dp": x * 2 + 1 - core}

    def owner_at(dz, dy):
        return lax.rem(z + n_z - dz, n_z) * n_y + lax.rem(y + n_y - dy, n_y)

    def z_peer(d):
        return {"group": lax.rem(z + d, n_z) * n_y + y}

    def y_peer(d):
        return {"group": z * n_y + lax.rem(y + d, n_y)}

    def g_peer(d):
        return {"group": lax.rem(me + d, n_g)}

    def rows(at, count):
        return pl.ds(pl.multiple_of(at, count), count)

    barrier = pltpu.get_barrier_semaphore()
    for d in range(1, n_x):
        pl.semaphore_signal(barrier, inc=1, device_id=x_peer(d), device_id_type=MESH)
    pl.semaphore_signal(barrier, inc=1, device_id=core_peer, device_id_type=MESH)
    for d in range(1, n_g):
        pl.semaphore_signal(barrier, inc=1, device_id=g_peer(d), device_id_type=MESH)
    pl.semaphore_wait(barrier, n_x - 1 + 1 + n_g - 1)

    def x_gather(buf, which, c, d):
        at = rows(share * block + c * part, part)
        return remote(buf.at[at], buf.at[at], gx_sems, (which, c, d - 1), x_peer(d))

    def core_gather(buf, which, c, d):
        at = rows(share_at(d, False) * block + c * part, part)
        return remote(buf.at[at], buf.at[at], gc_sems, (which, c, d), core_peer)

    gathered[rows(share * block, block), :] = embeds[...]
    for c in range(PARTS):
        for d in range(1, n_x):
            x_gather(gathered, 0, c, d).start()
        core_gather(gathered, 0, c, 0).start()

    def id_copy(d):
        return remote(ids.at[me], ids.at[me], id_sems, (d - 1,), g_peer(d))

    ids[me] = jnp.broadcast_to(own_ids[...], ids.shape[1:])
    for d in range(1, n_g):
        id_copy(d).start()

    def product(*places):
        value = jnp.concatenate([gathered[at, :] for at in places], 0)
        value = jnp.dot(value, w_first[...], preferred_element_type=jnp.float32)
        active = gelu_fwd(value).astype(jnp.bfloat16)
        count = value.shape[0] // len(places)
        for k, at in enumerate(places):
            pre[at, :] = value[k * count : (k + 1) * count]
            hidden[at, :] = active[k * count : (k + 1) * count]
        value = jnp.dot(active, w_second[...], preferred_element_type=jnp.float32)
        return value.astype(jnp.bfloat16)

    def core_sum(d, c):
        return remote(core_out.at[d, c], core_in.at[d, c], pc_sems, (d, c), core_peer)

    def x_sum(d, c):
        device = {"dp": share_at(d, False)}
        return remote(x_out.at[d - 1, c], x_in.at[d - 1, c], px_sems, (d - 1, c), device)

    def z_gather(p, d):
        at = rows(p * part, part)
        return remote(units.at[me, at], units.at[me, at], uz_sems, (p, d - 1), z_peer(d))

    def y_gather(p, dz, d):
        b, at = owner_at(dz, 0), rows(p * part, part)
        return remote(units.at[b, at], units.at[b, at], uy_sems, (p, dz, d - 1), y_peer(d))

    def normalise(c):
        at = rows(c * part, part)
        core_sum(0, c).wait_recv()
        proj = unit[at, :] + core_in[0, c].astype(jnp.float32)
        for d in range(1, n_x):
            x_sum(d, c).wait_recv()
            proj = proj + x_in[d - 1, c].astype(jnp.float32)
        inv = lax.rsqrt(jnp.mean(proj * proj, axis=-1, keepdims=True) + EPS)
        value = proj * inv
        inverse[at, :] = jnp.broadcast_to(inv, (part, LANES))
        unit[at, :] = value
        units[me, at, :] = value.astype(jnp.bfloat16)
        for d in range(1, n_z):
            z_gather(c, d).start()
        for d in range(1, n_y):
            y_gather(c, 0, d).start()

    def forward_embeds(c):
        for d in range(1, n_x):
            x_gather(gathered, 0, c, d).wait_recv()
            core_gather(gathered, 0, c, d).start()

    unit[...] = product(rows(share * block, block)).astype(jnp.float32)
    forward_embeds(0)
    for c in range(PARTS):
        core_gather(gathered, 0, c, 0).wait_recv()
    both = product(rows(share_at(0, True) * block, block))
    core_out[0] = both.reshape(core_out.shape[1:])
    for c in range(PARTS):
        core_sum(0, c).start()
    for c in range(PARTS):
        kept = []
        for d in range(1, n_x):
            core_gather(gathered, 0, c, d).wait_recv()
            both = product(
                rows(share_at(d, True) * block + c * part, part),
                rows(share_at(d, False) * block + c * part, part),
            )
            core_out[d, c] = both[:part]
            core_sum(d, c).start()
            kept.append(both[part:])
        if c + 1 < PARTS:
            forward_embeds(c + 1)
        for d in range(1, n_x):
            core_sum(d, c).wait_recv()
            own = kept[d - 1].astype(jnp.float32) + core_in[d, c].astype(jnp.float32)
            x_out[d - 1, c] = own.astype(jnp.bfloat16)
            x_sum(d, c).start()
        if c > 0:
            normalise(c - 1)
    normalise(PARTS - 1)

    for d in range(1, n_g):
        id_copy(d).wait_recv()
    grad_unit[...] = jnp.zeros(grad_unit.shape, jnp.float32)
    ids_col[...] = ids[me].T

    def add_block(b):
        logits = (
            TEMP
            / width_of(units)
            * lax.dot_general(
                units[me], units[b], (((1,), (1,)), ((), ())), preferred_element_type=jnp.float32
            )
            + SHIFT
        )
        sign = jnp.where(ids_col[:, 0:1] == ids[b][0:1, :], 1.0, -1.0).astype(jnp.float32)
        weight = (-sign * jax.nn.sigmoid(-sign * logits) * (TEMP / width_of(units))).astype(
            jnp.bfloat16
        )
        lists = (neighbors[pl.ds(me, 1), :] == b).astype(jnp.float32)
        listed_by = (neighbors[pl.ds(b, 1), :] == me).astype(jnp.float32)
        times = jnp.sum(lists + listed_by, axis=1, keepdims=True)
        times = jnp.where(b == me, 2.0, times)
        weight = (weight.astype(jnp.float32) * times).astype(jnp.bfloat16)
        grad_unit[...] += jnp.dot(weight, units[b], preferred_element_type=jnp.float32)

    add_block(me)

    @pl.loop(0, n_x * 2)
    def _(j):
        at = rows(j * block, block)
        gathered_t[:, at] = gathered[at, :].T

    for p in range(PARTS):
        for dz in range(1, n_z):
            z_gather(p, dz).wait_recv()
            for d in range(1, n_y):
                y_gather(p, dz, d).start()

    @pl.loop(1, n_z)
    def _(dz):
        add_block(owner_at(dz, 0))

    for dy in range(1, n_y):
        for p in range(PARTS):
            y_gather(p, 0, dy).wait_recv()
        add_block(owner_at(0, dy))

        @pl.loop(1, n_z)
        def _(dz, dy=dy):
            for p in range(PARTS):
                y_gather(p, dz, dy).wait_recv()
            add_block(owner_at(dz, dy))

    for c in range(PARTS):
        at = rows(c * part, part)
        total, value = grad_unit[at, :], unit[at, :]
        slope = jnp.mean(value * total, axis=-1, keepdims=True)
        grad = inverse[at, 0:1] * (total - value * slope)
        grad_all[rows(share * block + c * part, part), :] = grad.astype(jnp.bfloat16)
        for d in range(1, n_x):
            x_gather(grad_all, 1, c, d).start()
        core_gather(grad_all, 1, c, 0).start()

    def hand_out(j):
        at = rows(j * block, block)
        grads_t[:, at] = grad_all[at, :].T

    hand_out(share)
    for c in range(PARTS):
        for d in range(1, n_x):
            x_gather(grad_all, 1, c, d).wait_recv()
            core_gather(grad_all, 1, c, d).start()
    for d in range(n_x):
        if d > 0:
            hand_out(share_at(d, False))
        for c in range(PARTS):
            core_gather(grad_all, 1, c, d).wait_recv()
        hand_out(share_at(d, True))

    weight_part(
        n_y,
        n_z,
        grads_t,
        gathered_t,
        hidden,
        pre,
        grad_all,
        w_second,
        first,
        second,
        *weight_scratch,
    )

    for d in range(1, n_g):
        id_copy(d).wait_send()
    for c in range(PARTS):
        for which, buf in enumerate((gathered, grad_all)):
            for d in range(1, n_x):
                x_gather(buf, which, c, d).wait_send()
            for d in range(n_x):
                core_gather(buf, which, c, d).wait_send()
        for d in range(n_x):
            core_sum(d, c).wait_send()
        for d in range(1, n_x):
            x_sum(d, c).wait_send()

    for p in range(PARTS):
        for d in range(1, n_z):
            z_gather(p, d).wait_send()
        for d in range(1, n_y):
            for dz in range(n_z):
                y_gather(p, dz, d).wait_send()


def width_of(units):
    return units.shape[-1]


def step(embeds, row_ids, neighbors, w_first, w_second):
    owners, shares = lax.axis_size("group"), lax.axis_size("dp")
    n_y = split(owners, shares)
    n_z, n_x = owners // n_y, shares // 2
    block, wide = embeds.shape
    total, hid, width = shares * block, w_second.shape[0], w_second.shape[1]
    part, tall = block // PARTS, wide // owners
    items = 2 * (hid // CHUNK)
    vmem = pl.BlockSpec(memory_space=pltpu.VMEM)
    dma = pltpu.SemaphoreType.DMA
    bf16, f32, i16 = jnp.bfloat16, jnp.float32, jnp.int16
    return pl.pallas_call(
        functools.partial(step_kernel, n_x, n_y, n_z),
        out_shape=[
            jax.ShapeDtypeStruct((tall, hid), f32),
            jax.ShapeDtypeStruct((hid, tall), f32),
            jax.ShapeDtypeStruct((block, width), f32),
        ],
        in_specs=[vmem] * 5,
        out_specs=[vmem] * 3,
        scratch_shapes=[
            pltpu.VMEM((wide, total), bf16),
            pltpu.VMEM((total, hid), f32),
            pltpu.VMEM((total, hid), bf16),
            pltpu.VMEM((width, total), bf16),
            pltpu.VMEM((block, 8), jnp.int32),
            pltpu.VMEM((total, wide), bf16),
            pltpu.VMEM((owners, 8, block), jnp.int32),
            pltpu.VMEM((owners, block, width), bf16),
            pltpu.VMEM((block, width), f32),
            pltpu.VMEM((block, LANES), f32),
            pltpu.VMEM((total, width), bf16),
            pltpu.VMEM((n_x, PARTS, part, width), bf16),
            pltpu.VMEM((n_x, PARTS, part, width), bf16),
            pltpu.VMEM((n_x - 1, PARTS, part, width), bf16),
            pltpu.VMEM((n_x - 1, PARTS, part, width), bf16),
            dma((2, owners - 1)),
            dma((2, 2, PARTS, n_x - 1)),
            dma((2, 2, PARTS, n_x)),
            dma((2, n_x, PARTS)),
            dma((2, n_x - 1, PARTS)),
            dma((2, PARTS, n_z - 1)),
            dma((2, PARTS, n_z, n_y - 1)),
            pltpu.VMEM((total, CHUNK), bf16),
            pltpu.VMEM((items, n_z, tall, CHUNK), f32),
            pltpu.VMEM((items, tall, CHUNK), f32),
            pltpu.VMEM((items, n_y - 1, n_z, tall, CHUNK), i16),
            pltpu.VMEM((items, n_y - 1, n_z, tall, CHUNK), i16),
            pltpu.VMEM((items, n_y - 1, 8, LANES), f32),
            pltpu.VMEM((items, n_y - 1, 8, LANES), f32),
            pltpu.VMEM((items, n_z - 1, tall, CHUNK), i16),
            pltpu.VMEM((items, n_z - 1, tall, CHUNK), i16),
            pltpu.VMEM((items, n_z - 1, 8, LANES), f32),
            pltpu.VMEM((items, n_z - 1, 8, LANES), f32),
            dma((2, 2, items, n_y - 1)),
            dma((2, 2, items, n_z - 1)),
        ],
        compiler_params=pltpu.CompilerParams(
            collective_id=0, has_side_effects=True, vmem_limit_bytes=VMEM_BYTES
        ),
    )(embeds, row_ids[None, :], neighbors, w_first, w_second)


def per_device(embeds, row_ids, neighbors, w_first, w_second):
    return tuple(step(embeds, row_ids, neighbors, w_first, w_second))


def solution(mesh):
    in_specs = (
        P(("dp", "group"), None),
        P(("dp", "group")),
        P("dp", None),
        P(None, "dp"),
        P("dp", None),
    )
    out_specs = (P("group", "dp"), P("dp", "group"), P(("dp", "group"), None))
    return jax.shard_map(
        per_device, mesh=mesh, in_specs=in_specs, out_specs=out_specs, check_vma=False
    )
```

```python
import functools

import jax
import jax.numpy as jnp
from jax import lax
from jax.experimental import pallas as pl
from jax.experimental.pallas import tpu as pltpu
from jax.sharding import PartitionSpec as P

EPS = 1e-06
TEMP = 10.0
SHIFT = -5.0
LEVELS = 32000.0
LANES = 128
CHUNK = 256
PARTS = 4
VMEM_BYTES = 63 * 1024 * 1024
MESH = pl.DeviceIdType.MESH


def gelu_fwd(value):
    return jax.nn.gelu(value, approximate=True)


def gelu_back(pre, grad):
    _, back = jax.vjp(gelu_fwd, pre)
    return back(grad)[0]


def encode(value):
    flat = value.reshape(-1, value.shape[-1])
    top = jnp.max(jnp.abs(flat), axis=0, keepdims=True)
    joint = top[:, :LANES]
    for at in range(LANES, top.shape[1], LANES):
        joint = jnp.maximum(joint, top[:, at : at + LANES])
    joint = jnp.maximum(joint, 1e-30)
    inverse = jnp.tile(LEVELS / joint, (1, top.shape[1] // LANES))
    code = jnp.round(flat * inverse).astype(jnp.int32).astype(jnp.int16)
    return code.reshape(value.shape), jnp.broadcast_to(joint * (1.0 / LEVELS), (8, LANES))


def decode(code, scale):
    wide = jnp.tile(scale[0:1], (1, code.shape[-1] // LANES))
    return code.astype(jnp.int32).astype(jnp.float32) * wide


def weight_part(
    n_y,
    n_z,
    left0,
    left1,
    hidden,
    pre,
    grads,
    w_second,
    first,
    second,
    grad_pre,
    own,
    mine,
    y_out,
    y_in,
    y_scale_out,
    y_scale_in,
    z_out,
    z_in,
    z_scale_out,
    z_scale_in,
    y_sems,
    z_sems,
):
    me = lax.axis_index("group")
    z, y = me // n_y, me % n_y
    tall = first.shape[0]
    chunks = first.shape[1] // CHUNK

    def y_peer(d):
        return z * n_y + lax.rem(y + d, n_y)

    def z_peer(d):
        return lax.rem(z + d, n_z) * n_y + y

    def y_copies(i, d):
        return [
            pltpu.make_async_remote_copy(
                src_ref=a.at[i, d - 1],
                dst_ref=b.at[i, d - 1],
                send_sem=y_sems.at[which, 0, i, d - 1],
                recv_sem=y_sems.at[which, 1, i, d - 1],
                device_id={"group": y_peer(d)},
                device_id_type=MESH,
            )
            for which, (a, b) in enumerate(((y_out, y_in), (y_scale_out, y_scale_in)))
        ]

    def z_copies(i, d):
        return [
            pltpu.make_async_remote_copy(
                src_ref=a.at[i, d - 1],
                dst_ref=b.at[i, d - 1],
                send_sem=z_sems.at[which, 0, i, d - 1],
                recv_sem=z_sems.at[which, 1, i, d - 1],
                device_id={"group": z_peer(d)},
                device_id_type=MESH,
            )
            for which, (a, b) in enumerate(((z_out, z_in), (z_scale_out, z_scale_in)))
        ]

    def send_partials(i, left, rhs):
        def partial(owner_y, row):
            at = pl.multiple_of((row * n_y + owner_y) * tall, tall)
            return jnp.dot(left[pl.ds(at, tall), :], rhs, preferred_element_type=jnp.float32)

        for d in range(1, n_y):
            blocks = jnp.stack([partial(lax.rem(y + d, n_y), row) for row in range(n_z)])
            code, scale = encode(blocks)
            y_out[i, d - 1] = code
            y_scale_out[i, d - 1] = scale
            for copy in y_copies(i, d):
                copy.start()
        for row in range(n_z):
            own[i, row] = partial(y, row)

    def send_sums(i):
        for d in range(1, n_y):
            for copy in y_copies(i, d):
                copy.wait_recv()
        for d in range(1, n_z):
            row = lax.rem(z + d, n_z)
            block = own[i, row]
            for e in range(1, n_y):
                block = block + decode(y_in[i, e - 1, row], y_scale_in[i, e - 1])
            code, scale = encode(block)
            z_out[i, d - 1] = code
            z_scale_out[i, d - 1] = scale
            for copy in z_copies(i, d):
                copy.start()
        block = own[i, z]
        for e in range(1, n_y):
            block = block + decode(y_in[i, e - 1, z], y_scale_in[i, e - 1])
        mine[i] = block

    @pl.loop(0, chunks)
    def _(k):
        columns = pl.ds(pl.multiple_of(k * CHUNK, CHUNK), CHUNK)
        send_partials(k, left0, hidden[:, columns])

    @pl.loop(0, chunks)
    def _(k):
        columns = pl.ds(pl.multiple_of(k * CHUNK, CHUNK), CHUNK)
        w_rows = w_second[columns, :]

        @pl.loop(0, pre.shape[0] // CHUNK)
        def _(r):
            rows = pl.ds(pl.multiple_of(r * CHUNK, CHUNK), CHUNK)
            grad_hidden = lax.dot_general(
                grads[rows, :], w_rows, (((1,), (1,)), ((), ())), preferred_element_type=jnp.float32
            )
            grad_pre[rows, :] = gelu_back(pre[rows, columns], grad_hidden).astype(jnp.bfloat16)

        send_partials(chunks + k, left1, grad_pre[...])
        send_sums(k)

    @pl.loop(chunks, 2 * chunks)
    def _(i):
        send_sums(i)

    for m in range(2):

        @pl.loop(0, chunks)
        def _(k, m=m):
            i = m * chunks + k
            block = mine[i]
            for d in range(1, n_z):
                for copy in z_copies(i, d):
                    copy.wait_recv()
            for d in range(1, n_z):
                block = block + decode(z_in[i, d - 1], z_scale_in[i, d - 1])
            at = pl.ds(pl.multiple_of(k * CHUNK, CHUNK), CHUNK)
            if m == 0:
                second[at, :] = block.T
            else:
                first[:, at] = block

    @pl.loop(0, 2 * chunks)
    def _(i):
        for d in range(1, n_y):
            for copy in y_copies(i, d):
                copy.wait_send()
        for d in range(1, n_z):
            for copy in z_copies(i, d):
                copy.wait_send()


def split(owners, shares):
    return shares // 2 if owners % (shares // 2) == 0 else 1


def step_kernel(
    n_x,
    n_y,
    n_z,
    embeds,
    own_ids,
    neighbors,
    w_first,
    w_second,
    first,
    second,
    grad_unit,
    gathered_t,
    pre,
    hidden,
    grads_t,
    ids_col,
    gathered,
    ids,
    units,
    unit,
    inverse,
    grad_all,
    core_out,
    core_in,
    x_out,
    x_in,
    id_sems,
    gx_sems,
    gc_sems,
    pc_sems,
    px_sems,
    uz_sems,
    uy_sems,
    *weight_scratch,
):
    share, me = lax.axis_index("dp"), lax.axis_index("group")
    x, core = share // 2, share % 2
    z, y = me // n_y, me % n_y
    block, width = embeds.shape
    part = block // PARTS
    n_g = n_y * n_z

    def remote(src, dst, sems, at, device):
        return pltpu.make_async_remote_copy(
            src_ref=src,
            dst_ref=dst,
            send_sem=sems.at[(0,) + at],
            recv_sem=sems.at[(1,) + at],
            device_id=device,
            device_id_type=MESH,
        )

    def share_at(dx, other):
        return lax.rem(x + n_x - dx, n_x) * 2 + (1 - core if other else core)

    def x_peer(d):
        return {"dp": lax.rem(x + d, n_x) * 2 + core}

    core_peer = {"dp": x * 2 + 1 - core}

    def owner_at(dz, dy):
        return lax.rem(z + n_z - dz, n_z) * n_y + lax.rem(y + n_y - dy, n_y)

    def z_peer(d):
        return {"group": lax.rem(z + d, n_z) * n_y + y}

    def y_peer(d):
        return {"group": z * n_y + lax.rem(y + d, n_y)}

    def g_peer(d):
        return {"group": lax.rem(me + d, n_g)}

    def rows(at, count):
        return pl.ds(pl.multiple_of(at, count), count)

    barrier = pltpu.get_barrier_semaphore()
    for d in range(1, n_x):
        pl.semaphore_signal(barrier, inc=1, device_id=x_peer(d), device_id_type=MESH)
    pl.semaphore_signal(barrier, inc=1, device_id=core_peer, device_id_type=MESH)
    for d in range(1, n_g):
        pl.semaphore_signal(barrier, inc=1, device_id=g_peer(d), device_id_type=MESH)
    pl.semaphore_wait(barrier, n_x - 1 + 1 + n_g - 1)

    def x_gather(buf, which, c, d):
        at = rows(share * block + c * part, part)
        return remote(buf.at[at], buf.at[at], gx_sems, (which, c, d - 1), x_peer(d))

    def core_gather(buf, which, c, d):
        at = rows(share_at(d, False) * block + c * part, part)
        return remote(buf.at[at], buf.at[at], gc_sems, (which, c, d), core_peer)

    gathered[rows(share * block, block), :] = embeds[...]
    for c in range(PARTS):
        for d in range(1, n_x):
            x_gather(gathered, 0, c, d).start()
        core_gather(gathered, 0, c, 0).start()

    def id_copy(d):
        return remote(ids.at[me], ids.at[me], id_sems, (d - 1,), g_peer(d))

    ids[me] = jnp.broadcast_to(own_ids[...], ids.shape[1:])
    for d in range(1, n_g):
        id_copy(d).start()

    def product(*places):
        value = jnp.concatenate([gathered[at, :] for at in places], 0)
        value = jnp.dot(value, w_first[...], preferred_element_type=jnp.float32)
        active = gelu_fwd(value).astype(jnp.bfloat16)
        count = value.shape[0] // len(places)
        for k, at in enumerate(places):
            pre[at, :] = value[k * count : (k + 1) * count]
            hidden[at, :] = active[k * count : (k + 1) * count]
        value = jnp.dot(active, w_second[...], preferred_element_type=jnp.float32)
        return value.astype(jnp.bfloat16)

    def core_sum(d, c):
        return remote(core_out.at[d, c], core_in.at[d, c], pc_sems, (d, c), core_peer)

    def x_sum(d, c):
        device = {"dp": share_at(d, False)}
        return remote(x_out.at[d - 1, c], x_in.at[d - 1, c], px_sems, (d - 1, c), device)

    def line_copy(p, way, d):
        source = z - (d - 1) if way == 0 else z + (d - 1)
        to = lax.rem(z + (1 if way == 0 else n_z - 1), n_z)
        b, at = source * n_y + y, rows(p * part, part)
        device = {"group": to * n_y + y}
        return remote(units.at[b, at], units.at[b, at], uz_sems, (way, p, d - 1), device)

    def arrives(way, d):
        return z >= d if way == 0 else z + d < n_z

    def leaves(way, d):
        if way == 0:
            return jnp.logical_and(z >= d - 1, z + 1 < n_z)
        return jnp.logical_and(z + d - 1 < n_z, z >= 1)

    def relay(p):
        for d in range(1, n_z):
            for way in range(2):

                @pl.when(arrives(way, d))
                def _(d=d, way=way):
                    line_copy(p, way, d).wait_recv()
                    for e in range(1, n_y):
                        y_gather(p, d if way == 0 else n_z - d, e).start()

                if d + 1 < n_z:

                    @pl.when(jnp.logical_and(arrives(way, d), leaves(way, d + 1)))
                    def _(d=d, way=way):
                        line_copy(p, way, d + 1).start()

    def y_gather(p, dz, d):
        b, at = owner_at(dz, 0), rows(p * part, part)
        return remote(units.at[b, at], units.at[b, at], uy_sems, (p, dz, d - 1), y_peer(d))

    def normalise(c):
        at = rows(c * part, part)
        core_sum(0, c).wait_recv()
        proj = unit[at, :] + core_in[0, c].astype(jnp.float32)
        for d in range(1, n_x):
            x_sum(d, c).wait_recv()
            proj = proj + x_in[d - 1, c].astype(jnp.float32)
        inv = lax.rsqrt(jnp.mean(proj * proj, axis=-1, keepdims=True) + EPS)
        value = proj * inv
        inverse[at, :] = jnp.broadcast_to(inv, (part, LANES))
        unit[at, :] = value
        units[me, at, :] = value.astype(jnp.bfloat16)
        for way in range(2):

            @pl.when(leaves(way, 1))
            def _(way=way):
                line_copy(c, way, 1).start()

        for d in range(1, n_y):
            y_gather(c, 0, d).start()

    def forward_embeds(c):
        for d in range(1, n_x):
            x_gather(gathered, 0, c, d).wait_recv()
            core_gather(gathered, 0, c, d).start()

    unit[...] = product(rows(share * block, block)).astype(jnp.float32)
    forward_embeds(0)
    for c in range(PARTS):
        core_gather(gathered, 0, c, 0).wait_recv()
    both = product(rows(share_at(0, True) * block, block))
    core_out[0] = both.reshape(core_out.shape[1:])
    for c in range(PARTS):
        core_sum(0, c).start()
    for c in range(PARTS):
        kept = []
        for d in range(1, n_x):
            core_gather(gathered, 0, c, d).wait_recv()
            both = product(
                rows(share_at(d, True) * block + c * part, part),
                rows(share_at(d, False) * block + c * part, part),
            )
            core_out[d, c] = both[:part]
            core_sum(d, c).start()
            kept.append(both[part:])
        if c + 1 < PARTS:
            forward_embeds(c + 1)
        for d in range(1, n_x):
            core_sum(d, c).wait_recv()
            own = kept[d - 1].astype(jnp.float32) + core_in[d, c].astype(jnp.float32)
            x_out[d - 1, c] = own.astype(jnp.bfloat16)
            x_sum(d, c).start()
        if c > 0:
            normalise(c - 1)
    normalise(PARTS - 1)

    for d in range(1, n_g):
        id_copy(d).wait_recv()
    grad_unit[...] = jnp.zeros(grad_unit.shape, jnp.float32)
    ids_col[...] = ids[me].T

    def add_block(b):
        logits = (
            TEMP
            / width_of(units)
            * lax.dot_general(
                units[me], units[b], (((1,), (1,)), ((), ())), preferred_element_type=jnp.float32
            )
            + SHIFT
        )
        sign = jnp.where(ids_col[:, 0:1] == ids[b][0:1, :], 1.0, -1.0).astype(jnp.float32)
        weight = (-sign * jax.nn.sigmoid(-sign * logits) * (TEMP / width_of(units))).astype(
            jnp.bfloat16
        )
        lists = (neighbors[pl.ds(me, 1), :] == b).astype(jnp.float32)
        listed_by = (neighbors[pl.ds(b, 1), :] == me).astype(jnp.float32)
        times = jnp.sum(lists + listed_by, axis=1, keepdims=True)
        times = jnp.where(b == me, 2.0, times)
        weight = (weight.astype(jnp.float32) * times).astype(jnp.bfloat16)
        grad_unit[...] += jnp.dot(weight, units[b], preferred_element_type=jnp.float32)

    turns = -(-2 * n_x // PARTS)
    for p in range(PARTS):
        relay(p)

        @pl.loop(p * turns, min((p + 1) * turns, 2 * n_x))
        def _(j):
            at = rows(j * block, block)
            gathered_t[:, at] = gathered[at, :].T

    add_block(me)

    @pl.loop(1, n_z)
    def _(dz):
        add_block(owner_at(dz, 0))

    for dy in range(1, n_y):
        for p in range(PARTS):
            y_gather(p, 0, dy).wait_recv()
        add_block(owner_at(0, dy))

        @pl.loop(1, n_z)
        def _(dz, dy=dy):
            for p in range(PARTS):
                y_gather(p, dz, dy).wait_recv()
            add_block(owner_at(dz, dy))

    for c in range(PARTS):
        at = rows(c * part, part)
        total, value = grad_unit[at, :], unit[at, :]
        slope = jnp.mean(value * total, axis=-1, keepdims=True)
        grad = inverse[at, 0:1] * (total - value * slope)
        grad_all[rows(share * block + c * part, part), :] = grad.astype(jnp.bfloat16)
        for d in range(1, n_x):
            x_gather(grad_all, 1, c, d).start()
        core_gather(grad_all, 1, c, 0).start()

    def hand_out(j):
        at = rows(j * block, block)
        grads_t[:, at] = grad_all[at, :].T

    hand_out(share)
    for c in range(PARTS):
        for d in range(1, n_x):
            x_gather(grad_all, 1, c, d).wait_recv()
            core_gather(grad_all, 1, c, d).start()
    for d in range(n_x):
        if d > 0:
            hand_out(share_at(d, False))
        for c in range(PARTS):
            core_gather(grad_all, 1, c, d).wait_recv()
        hand_out(share_at(d, True))

    weight_part(
        n_y,
        n_z,
        grads_t,
        gathered_t,
        hidden,
        pre,
        grad_all,
        w_second,
        first,
        second,
        *weight_scratch,
    )

    for d in range(1, n_g):
        id_copy(d).wait_send()
    for c in range(PARTS):
        for which, buf in enumerate((gathered, grad_all)):
            for d in range(1, n_x):
                x_gather(buf, which, c, d).wait_send()
            for d in range(n_x):
                core_gather(buf, which, c, d).wait_send()
        for d in range(n_x):
            core_sum(d, c).wait_send()
        for d in range(1, n_x):
            x_sum(d, c).wait_send()

    for p in range(PARTS):
        for d in range(1, n_z):
            for way in range(2):

                @pl.when(leaves(way, d))
                def _(p=p, d=d, way=way):
                    line_copy(p, way, d).wait_send()

        for d in range(1, n_y):
            for dz in range(n_z):
                y_gather(p, dz, d).wait_send()


def width_of(units):
    return units.shape[-1]


def step(embeds, row_ids, neighbors, w_first, w_second):
    owners, shares = lax.axis_size("group"), lax.axis_size("dp")
    n_y = split(owners, shares)
    n_z, n_x = owners // n_y, shares // 2
    block, wide = embeds.shape
    total, hid, width = shares * block, w_second.shape[0], w_second.shape[1]
    part, tall = block // PARTS, wide // owners
    items = 2 * (hid // CHUNK)
    vmem = pl.BlockSpec(memory_space=pltpu.VMEM)
    dma = pltpu.SemaphoreType.DMA
    bf16, f32, i16 = jnp.bfloat16, jnp.float32, jnp.int16
    return pl.pallas_call(
        functools.partial(step_kernel, n_x, n_y, n_z),
        out_shape=[
            jax.ShapeDtypeStruct((tall, hid), f32),
            jax.ShapeDtypeStruct((hid, tall), f32),
            jax.ShapeDtypeStruct((block, width), f32),
        ],
        in_specs=[vmem] * 5,
        out_specs=[vmem] * 3,
        scratch_shapes=[
            pltpu.VMEM((wide, total), bf16),
            pltpu.VMEM((total, hid), f32),
            pltpu.VMEM((total, hid), bf16),
            pltpu.VMEM((width, total), bf16),
            pltpu.VMEM((block, 8), jnp.int32),
            pltpu.VMEM((total, wide), bf16),
            pltpu.VMEM((owners, 8, block), jnp.int32),
            pltpu.VMEM((owners, block, width), bf16),
            pltpu.VMEM((block, width), f32),
            pltpu.VMEM((block, LANES), f32),
            pltpu.VMEM((total, width), bf16),
            pltpu.VMEM((n_x, PARTS, part, width), bf16),
            pltpu.VMEM((n_x, PARTS, part, width), bf16),
            pltpu.VMEM((n_x - 1, PARTS, part, width), bf16),
            pltpu.VMEM((n_x - 1, PARTS, part, width), bf16),
            dma((2, owners - 1)),
            dma((2, 2, PARTS, n_x - 1)),
            dma((2, 2, PARTS, n_x)),
            dma((2, n_x, PARTS)),
            dma((2, n_x - 1, PARTS)),
            dma((2, 2, PARTS, n_z - 1)),
            dma((2, PARTS, n_z, n_y - 1)),
            pltpu.VMEM((total, CHUNK), bf16),
            pltpu.VMEM((items, n_z, tall, CHUNK), f32),
            pltpu.VMEM((items, tall, CHUNK), f32),
            pltpu.VMEM((items, n_y - 1, n_z, tall, CHUNK), i16),
            pltpu.VMEM((items, n_y - 1, n_z, tall, CHUNK), i16),
            pltpu.VMEM((items, n_y - 1, 8, LANES), f32),
            pltpu.VMEM((items, n_y - 1, 8, LANES), f32),
            pltpu.VMEM((items, n_z - 1, tall, CHUNK), i16),
            pltpu.VMEM((items, n_z - 1, tall, CHUNK), i16),
            pltpu.VMEM((items, n_z - 1, 8, LANES), f32),
            pltpu.VMEM((items, n_z - 1, 8, LANES), f32),
            dma((2, 2, items, n_y - 1)),
            dma((2, 2, items, n_z - 1)),
        ],
        compiler_params=pltpu.CompilerParams(
            collective_id=0, has_side_effects=True, vmem_limit_bytes=VMEM_BYTES
        ),
    )(embeds, row_ids[None, :], neighbors, w_first, w_second)


def per_device(embeds, row_ids, neighbors, w_first, w_second):
    return tuple(step(embeds, row_ids, neighbors, w_first, w_second))


def solution(mesh):
    in_specs = (
        P(("dp", "group"), None),
        P(("dp", "group")),
        P("dp", None),
        P(None, "dp"),
        P("dp", None),
    )
    out_specs = (P("group", "dp"), P("dp", "group"), P(("dp", "group"), None))
    return jax.shard_map(
        per_device, mesh=mesh, in_specs=in_specs, out_specs=out_specs, check_vma=False
    )
```
